512 devices in a mesh: cp: 64 (over x, y, z_hi), hd: 8 (over z_lo, core).
Axes of the slice: x: 4, y: 4, z: 16 (z_hi: 4, z_lo: 4; z = z_hi * 4 + z_lo), core: 2. Of those that a mesh axis runs over, the one named last changes fastest.
Arguments:
- queries: bfloat16 [32768, 8192], P(('cp', 'hd')), may hold values from -8 to 8
- key_vectors: bfloat16 [32768, 1024], P(('cp', 'hd')), may hold values from -8 to 8
- value_vectors: bfloat16 [32768, 1024], P(('cp', 'hd')), may hold values from -6 to 6
- out_grad: bfloat16 [32768, 8192], P(('cp', 'hd')), may hold values from -6 to 6
- doc_lengths: int32 [128], replicated, may hold values from 1 to 512, 32768 in all
Outputs:
- attended: bfloat16 [32768, 8192], P(('cp', 'hd'))
- query_grad: bfloat16 [32768, 8192], P(('cp', 'hd'))
- key_grad: bfloat16 [32768, 1024], P(('cp', 'hd'))
- value_grad: bfloat16 [32768, 1024], P(('cp', 'hd'))
The draws below stay inside these ranges and needn't reach their ends.
Inputs may be any that keep to these rules, and one draw needn't show every extreme that they name: `doc_lengths`: the lengths sum to 32768; the longest document has exactly 512 tokens.
All inputs are finite; a program needn't handle non-finite values.
Results may differ from the reference program's by a relative error of at most 0.027.
Values may be sent and summed in bfloat16 or wider, within the bound.
A program may use at most 128 MiB of HBM per device.

```python
import math
import jax
import jax.numpy as jnp
import numpy as np
from jax import lax

HQ = 64
HK = 8
DH = 128
TOK_DEV = 512
SPAN = 1
TOKENS = 32768
DOC_MAX = 512
NDOCS = 128


def draw_queries(key, part):
    key = jax.random.fold_in(key, 11)
    drawn_draw = jnp.clip(jax.random.normal(key, (TOKENS, HK, HQ // HK, DH), jnp.float32), -6.0, 6.0)
    return drawn_draw.reshape(TOKENS, HQ * DH).astype(jnp.bfloat16)


def draw_key_vectors(key, part):
    key = jax.random.fold_in(key, 12)
    drawn_draw = jnp.clip(jax.random.normal(key, (TOKENS, HK, DH), jnp.float32), -6.0, 6.0)
    return drawn_draw.reshape(TOKENS, HK * DH).astype(jnp.bfloat16)


def shard_levels(own_key, dims, shards, least, high):
    def one(axis_at, shards_of):
        heights = jax.random.uniform(jax.random.fold_in(jax.random.fold_in(own_key, 6), axis_at), (shards_of,), jnp.float32, least / len(shards), high / len(shards))
        return jnp.repeat(jnp.exp(heights), dims[axis_at] // shards_of).reshape((-1,) + (1,) * (len(dims) - axis_at - 1))

    gain = one(*shards[0])
    for cut in shards[1:]:
        gain = gain * one(*cut)
    return gain


def profile(count, total, most, slope):
    loads = [(1 << 20) // math.isqrt(grade ** slope) + 1 for grade in range(2, count + 1)]
    surplus, counts = total - most - (count - 1), [1] * (count - 1)
    while surplus > 0:
        movable = [i for i in range(count - 1) if counts[i] < most]
        mass, budget = sum([loads[i] for i in movable]), surplus
        for i in movable:
            addition = min(most - counts[i], max(1, budget * loads[i] // mass), surplus)
            counts[i] = counts[i] + addition
            surplus = surplus - addition
    return np.array([most] + counts)


def uneven(rng, number_of, total, most, skew):
    if number_of == 2:
        one = jax.random.randint(rng, (), max(1, total - most), min(most, total - 1) + 1)
        return jnp.stack([one, total - one])
    sizes = jnp.asarray(profile(number_of, total, most, skew), jnp.int32)
    twos = (number_of - 1) // 2
    source_of, taker = sizes[1:1 + 2 * twos:2], sizes[2:2 + 2 * twos:2]
    margin = jnp.minimum(source_of - 1, most - taker)
    moved = jax.random.randint(jax.random.fold_in(rng, 1), (twos,), 0, 1 << 20) % (margin + 1)
    sizes = sizes.at[1:1 + 2 * twos:2].set(source_of - moved).at[2:2 + 2 * twos:2].set(taker + moved)
    return sizes[jax.random.permutation(jax.random.fold_in(rng, 2), number_of)]


def bell_draw(own_key, dims, deviation, most, cuts=(), kind=jnp.bfloat16):
    entries = deviation * jax.random.normal(own_key, dims, jnp.float32)
    if cuts:
        entries = entries * shard_levels(own_key, dims, cuts, -0.22, 0.18)
    return jnp.clip(entries, -most, most).astype(kind)


def setup_inputs(seed: int = 0) -> dict:
    keys = jax.random.split(jax.random.key(seed), 6)
    return {
        "queries": draw_queries(jax.random.fold_in(keys[5], 71), 0),
        "key_vectors": draw_key_vectors(jax.random.fold_in(keys[5], 71), 0),
        "value_vectors": bell_draw(keys[2], (TOKENS, HK * DH), 1.0, 6.0, ((0, 512),)),
        "out_grad": bell_draw(keys[3], (TOKENS, HQ * DH), 1.0, 6.0, ((0, 512),)),
        "doc_lengths": uneven(keys[4], NDOCS, TOKENS, DOC_MAX, 2).astype(jnp.int32),
    }


def segment_of(positions, doc_lengths):
    doc_ends = jnp.cumsum(doc_lengths).astype(jnp.int32)
    return jnp.sum((doc_ends[None, :] <= positions[:, None]).astype(jnp.int32), axis=1)


def reference(queries, key_vectors, value_vectors, out_grad, doc_lengths):
    score_scale = DH ** -0.5
    group_size = HQ // HK
    window_rows = (SPAN + 1) * TOK_DEV
    blocks = TOKENS // TOK_DEV
    pad_rows = SPAN * TOK_DEV
    keys_pad = jnp.concatenate([jnp.zeros((pad_rows, HK * DH), jnp.bfloat16), key_vectors], 0)
    values_pad = jnp.concatenate([jnp.zeros((pad_rows, HK * DH), jnp.bfloat16), value_vectors], 0)

    def one_block(carried, block_index):
        key_total, value_total = carried
        row_start = (block_index * TOK_DEV).astype(jnp.int32)
        query_heads = lax.dynamic_slice_in_dim(queries, row_start, TOK_DEV, 0).reshape(TOK_DEV, HK, group_size, DH).astype(jnp.float32)
        grad_heads = lax.dynamic_slice_in_dim(out_grad, row_start, TOK_DEV, 0).reshape(TOK_DEV, HK, group_size, DH).astype(jnp.float32)
        key_window = lax.dynamic_slice_in_dim(keys_pad, row_start, window_rows, 0).reshape(SPAN + 1, TOK_DEV, HK, DH).astype(jnp.float32)
        value_window = lax.dynamic_slice_in_dim(values_pad, row_start, window_rows, 0).reshape(SPAN + 1, TOK_DEV, HK, DH).astype(jnp.float32)
        query_pos = row_start + jnp.arange(TOK_DEV, dtype=jnp.int32)
        key_pos = row_start - pad_rows + jnp.arange(window_rows, dtype=jnp.int32)
        query_seg = segment_of(query_pos, doc_lengths)
        key_seg = segment_of(key_pos, doc_lengths).reshape(SPAN + 1, TOK_DEV)
        key_pos = key_pos.reshape(SPAN + 1, TOK_DEV)
        allowed = (key_pos[None] >= 0) & (key_pos[None] <= query_pos[:, None, None]) & (key_seg[None] == query_seg[:, None, None])
        allowed = allowed[:, None, None, :, :]
        scores = jnp.einsum('thgd,jshd->thgjs', query_heads, key_window) * score_scale
        block_max = jnp.max(jnp.where(allowed, scores, -1e30), axis=-1)
        weights = jnp.where(allowed, jnp.exp(scores - block_max[..., None]), 0.0)
        block_sum = jnp.sum(weights, axis=-1)
        rounded_weights = weights.astype(jnp.bfloat16).astype(jnp.float32)
        partial_value = jnp.einsum('thgjs,jshd->thgjd', rounded_weights, value_window)
        run_max = jnp.max(block_max, axis=-1)
        factor = jnp.exp(block_max - run_max[..., None])
        norm_sum = jnp.sum(factor * block_sum, axis=-1)
        out_heads = (jnp.sum(factor[..., None] * partial_value, axis=3) / norm_sum[..., None]).astype(jnp.bfloat16)
        log_norm = run_max + jnp.log(norm_sum)
        out_dot = jnp.sum(grad_heads * out_heads.astype(jnp.float32), axis=-1)
        probabilities = jnp.where(allowed, jnp.exp(scores - log_norm[..., None, None]), 0.0)
        prob_grad = jnp.einsum('thgd,jshd->thgjs', grad_heads, value_window)
        score_grad = probabilities * (prob_grad - out_dot[..., None, None])
        rounded_probs = probabilities.astype(jnp.bfloat16).astype(jnp.float32)
        rounded_grads = score_grad.astype(jnp.bfloat16).astype(jnp.float32)
        query_part = (jnp.einsum('thgjs,jshd->thgd', rounded_grads, key_window) * score_scale).astype(jnp.bfloat16)
        key_part = (jnp.einsum('thgjs,thgd->jshd', rounded_grads, query_heads) * score_scale).reshape(window_rows, HK * DH)
        value_part = jnp.einsum('thgjs,thgd->jshd', rounded_probs, grad_heads).reshape(window_rows, HK * DH)
        key_total = lax.dynamic_update_slice_in_dim(key_total, lax.dynamic_slice_in_dim(key_total, row_start, window_rows, 0) + key_part, row_start, 0)
        value_total = lax.dynamic_update_slice_in_dim(value_total, lax.dynamic_slice_in_dim(value_total, row_start, window_rows, 0) + value_part, row_start, 0)
        return (key_total, value_total), (out_heads.reshape(TOK_DEV, HQ * DH), query_part.reshape(TOK_DEV, HQ * DH))

    zero_grads = jnp.zeros((TOKENS + pad_rows, HK * DH), jnp.float32)
    (key_total, value_total), (out_blocks, grad_blocks) = lax.scan(one_block, (zero_grads, zero_grads), jnp.arange(blocks, dtype=jnp.int32))
    attended = out_blocks.reshape(TOKENS, HQ * DH)
    query_grad = grad_blocks.reshape(TOKENS, HQ * DH)
    return attended, query_grad, key_total[pad_rows:].astype(jnp.bfloat16), value_total[pad_rows:].astype(jnp.bfloat16)
```

```python
import functools
import math

import jax
import jax.numpy as jnp
from jax import lax
from jax.experimental import pallas as pl
from jax.experimental.pallas import tpu as pltpu
from jax.sharding import PartitionSpec as P

DH = 128
ROWS = 64
CHIP = 2 * ROWS
SLOTS = 5
KEYS = SLOTS * CHIP
HEADS = 4
GROUP = 8
WIDE = GROUP * DH
PAIR = 2 * CHIP
SCALE = DH ** (-0.5)
MESH = pl.DeviceIdType.MESH
F32 = jnp.float32
BF16 = jnp.bfloat16


def kernel(
    devices,
    q_in, k_in, v_in, g_in, len_in,
    att_out, dq_out, dk_out, dv_out,
    kv, qb, gb, ob, dqb, acc, gin, gout, fin, bias, lens,
    key_pair, key_t, value_pair, value_t, scores, weights, probs, changes,
    len_sem, kv_recv, kv_fwd, own_ici, own_sib,
    qg_recv, qg_send, sum_recv, sum_send,
    out_loc, out_send, out_recv, fin_loc, fin_send, fin_recv,
):
    cp = lax.axis_index("cp")
    hd = lax.axis_index("hd")
    me = cp * 8 + hd
    core = lax.rem(hd, 2)
    other = 1 - core

    def device(index):
        index = lax.rem(index + devices, devices)
        return (index // 8, lax.rem(index, 8))

    sibling = (cp, hd + 1 - 2 * core)
    chip_base = me - core
    ahead = device(me + 2)
    ahead_other = device(chip_base + 2 + other)
    behind = device(me - 2)
    behind_other = device(chip_base - 2 + other)
    my_rows = pl.ds(pl.multiple_of(core * ROWS, ROWS), ROWS)
    sib_rows = pl.ds(pl.multiple_of(other * ROWS, ROWS), ROWS)

    def head_cols(owner, h, width):
        return pl.ds(pl.multiple_of((owner * HEADS + h) * width, width), width)

    def remote(src, dst, send, recv, target):
        return pltpu.make_async_remote_copy(
            src_ref=src, dst_ref=dst, send_sem=send, recv_sem=recv, device_id=target, device_id_type=MESH
        )

    def own_to_ahead(h):
        made = []
        for side, (owner, target) in enumerate(((core, ahead), (other, ahead_other))):
            for part, src in enumerate((k_in, v_in)):
                made.append(remote(
                    src.at[:, head_cols(owner, h, DH)], kv.at[h, 3, part, my_rows],
                    own_ici.at[h, side, part], kv_recv.at[h, 3], target,
                ))
        return made

    def own_to_sibling(h):
        return [
            remote(src.at[:, head_cols(other, h, DH)], kv.at[h, 4, part, my_rows],
                   own_sib.at[h, part], kv_recv.at[h, 4], sibling)
            for part, src in enumerate((k_in, v_in))
        ]

    def own_local(h):
        return [
            pltpu.make_async_copy(src.at[:, head_cols(core, h, DH)], kv.at[h, 4, part, my_rows], kv_recv.at[h, 4])
            for part, src in enumerate((k_in, v_in))
        ]

    def rows_to_sibling(h):
        return [
            remote(src.at[:, head_cols(other, h, WIDE)], dst.at[h, my_rows],
                   qg_send.at[h, part], qg_recv.at[h, part], sibling)
            for part, (src, dst) in enumerate(((q_in, qb), (g_in, gb)))
        ]

    def rows_local(h):
        return [
            pltpu.make_async_copy(src.at[:, head_cols(core, h, WIDE)], dst.at[h, my_rows], qg_recv.at[h, part])
            for part, (src, dst) in enumerate(((q_in, qb), (g_in, gb)))
        ]

    def start(copies):
        for copy in copies:
            copy.start()

    def wait_kv(h, slot):
        pltpu.make_async_copy(kv.at[h, slot], kv.at[h, slot], kv_recv.at[h, slot]).wait()

    def wait_rows(h):
        for part, dst in enumerate((qb, gb)):
            pltpu.make_async_copy(dst.at[h], dst.at[h], qg_recv.at[h, part]).wait()

    def forward(h, slot):
        return remote(kv.at[h, slot], kv.at[h, slot - 1], kv_fwd.at[h, slot - 1], kv_recv.at[h, slot - 1], ahead)

    def own_ahead(h):
        start(own_to_ahead(h))

    def pass_on(h, slot):
        wait_kv(h, slot)
        forward(h, slot).start()

    def sum_copy(h, slot):
        return remote(gout.at[h, slot], gin.at[h, slot], sum_send.at[h, slot], sum_recv.at[h, slot], behind)

    def first_sum(h):
        for part in range(2):
            gout[h, 0, part] = acc[h, part, 0:CHIP].astype(BF16)
        sum_copy(h, 0).start()

    def next_sum(h, slot):
        pltpu.make_async_copy(gin.at[h, slot - 1], gin.at[h, slot - 1], sum_recv.at[h, slot - 1]).wait()
        for part in range(2):
            total = gin[h, slot - 1, part].astype(F32) + acc[h, part, slot * CHIP:(slot + 1) * CHIP]
            if slot < 4:
                gout[h, slot, part] = total.astype(BF16)
            else:
                fin[h, part] = total.astype(BF16)
        if slot < 4:
            sum_copy(h, slot).start()
        else:
            start(fin_local(h))
            start(fin_remote(h))

    def fin_local(h):
        return [
            pltpu.make_async_copy(fin.at[h, part, my_rows], dst.at[:, head_cols(core, h, DH)], fin_loc.at[h, part])
            for part, dst in enumerate((dk_out, dv_out))
        ]

    def fin_remote(h):
        return [
            remote(fin.at[h, part, sib_rows], dst.at[:, head_cols(core, h, DH)],
                   fin_send.at[h, part], fin_recv.at[h, part], sibling)
            for part, dst in enumerate((dk_out, dv_out))
        ]

    def out_local(h):
        return [
            pltpu.make_async_copy(src.at[h, my_rows], dst.at[:, head_cols(core, h, WIDE)], out_loc.at[h, part])
            for part, (src, dst) in enumerate(((ob, att_out), (dqb, dq_out)))
        ]

    def out_remote(h):
        return [
            remote(src.at[h, sib_rows], dst.at[:, head_cols(core, h, WIDE)],
                   out_send.at[h, part], out_recv.at[h, part], sibling)
            for part, (src, dst) in enumerate(((ob, att_out), (dqb, dq_out)))
        ]

    barrier = pltpu.get_barrier_semaphore()
    for peer in (sibling, ahead, ahead_other, behind, behind_other):
        pl.semaphore_signal(barrier, inc=1, device_id=peer, device_id_type=MESH)
    len_copy = pltpu.make_async_copy(len_in, lens, len_sem)
    len_copy.start()
    for h in range(HEADS):
        start(own_local(h))
    for h in range(HEADS):
        start(rows_local(h))
    pl.semaphore_wait(barrier, 5)

    start(own_to_ahead(0))
    start(own_to_ahead(1))
    for h in range(HEADS):
        start(own_to_sibling(h))
    start(rows_to_sibling(0))

    len_copy.wait()
    first_pos = (chip_base // 2) * CHIP
    low = lax.broadcasted_iota(jnp.int32, (DH, DH), 0)
    high = lax.broadcasted_iota(jnp.int32, (DH, DH), 1)
    ends_col = jnp.sum(jnp.where(high <= low, lens[...].astype(F32), 0.0), axis=1, keepdims=True)
    ends_row = jnp.sum(jnp.where(low == high, ends_col, 0.0), axis=0, keepdims=True)
    query_pos = high + first_pos
    query_seg = jnp.sum(jnp.where(ends_col <= query_pos.astype(F32), 1.0, 0.0), axis=0, keepdims=True)
    for slot in range(SLOTS):
        key_pos = low + (first_pos - (4 - slot) * CHIP)
        key_seg = jnp.sum(jnp.where(ends_row <= key_pos.astype(F32), 1.0, 0.0), axis=1, keepdims=True)
        allowed = (key_pos >= 0) & (key_pos <= query_pos) & (key_seg == query_seg)
        bias[slot * CHIP:(slot + 1) * CHIP, :] = jnp.where(allowed, 0.0, -1e30)

    pass_on(0, 3)
    start(rows_to_sibling(1))
    pass_on(1, 3)
    pass_on(0, 2)
    start(rows_to_sibling(2))
    pass_on(1, 2)
    pass_on(0, 1)
    start(own_to_ahead(2))
    start(rows_to_sibling(3))
    pass_on(1, 1)

    lane = lax.broadcasted_iota(jnp.int32, (PAIR, DH), 1)
    key_lane = lax.broadcasted_iota(jnp.int32, (KEYS, DH), 1)
    value_pair[:, DH:] = jnp.where(key_lane < 2, -1.0, 0.0).astype(BF16)
    value_t[DH:, :] = jnp.ones((16, KEYS), BF16)
    blocks = [slice(slot * CHIP, (slot + 1) * CHIP) for slot in range(SLOTS)]
    across = (((1,), (1,)), ((), ()))

    def prepare(h):
        keys = kv[h, :, 0].reshape(KEYS, DH)
        values = kv[h, :, 1].reshape(KEYS, DH)
        key_t[...] = keys.T
        value_t[:DH, :] = values.T
        value_pair[:, :DH] = values
        scaled = keys.astype(F32) * (SCALE * math.log2(math.e))
        scaled_top = scaled.astype(BF16)
        key_pair[:, :DH] = scaled_top
        key_pair[:, DH:] = (scaled - scaled_top.astype(F32)).astype(BF16)

    def chunk(h, p):
        cols = [slice((2 * p + i) * DH, (2 * p + i + 1) * DH) for i in range(2)]
        pair = slice(p * PAIR, (p + 1) * PAIR)
        query = jnp.concatenate([qb[h, :, c] for c in cols], axis=0)
        query = jnp.concatenate([query, query], axis=1)
        top = None
        for block in blocks:
            one_bias = bias[block]
            part = lax.dot_general(key_pair[block], query, across, preferred_element_type=F32)
            part = part + jnp.concatenate([one_bias, one_bias], axis=1)
            scores[block] = part
            part = jnp.max(part.reshape(CHIP // 8, 8, PAIR), axis=0)
            top = part if top is None else jnp.maximum(top, part)
        top = jnp.max(top, axis=0, keepdims=True)
        for block in blocks:
            weights[block] = jnp.exp2(scores[block] - top).astype(BF16)
        out = jnp.dot(value_t[...], weights[...], preferred_element_type=F32)
        inverse = 1.0 / out[DH:DH + 1]
        out = (out[:DH] * inverse).T.astype(BF16)
        grad = jnp.concatenate([gb[h, :, c] for c in cols], axis=0)
        for i, c in enumerate(cols):
            ob[h, :, c] = out[i * CHIP:(i + 1) * CHIP]
        delta = jnp.sum(out.astype(F32) * grad.astype(F32), axis=1, keepdims=True)
        delta_top = delta.astype(BF16).astype(F32)
        tail = jnp.where(lane == 0, delta_top, jnp.where(lane == 1, delta - delta_top, 0.0)).astype(BF16)
        grad = jnp.concatenate([grad, tail], axis=1)
        inverse = jnp.broadcast_to(inverse, (CHIP, PAIR)).astype(BF16)
        for block in blocks:
            change = lax.dot_general(value_pair[block], grad, across, preferred_element_type=F32).astype(BF16)
            prob = weights[block] * inverse
            probs[block, pair] = prob
            changes[block, pair] = prob * change
        query_grad = (jnp.dot(key_t[...], changes[:, pair], preferred_element_type=F32) * SCALE).T.astype(BF16)
        for i, c in enumerate(cols):
            dqb[h, :, c] = query_grad[i * CHIP:(i + 1) * CHIP]

    def key_sums(h):
        query = jnp.concatenate([qb[h, :, g * DH:(g + 1) * DH] for g in range(GROUP)], axis=0)
        acc[h, 0] = jnp.dot(changes[...], query, preferred_element_type=F32) * SCALE
        grad = jnp.concatenate([gb[h, :, g * DH:(g + 1) * DH] for g in range(GROUP)], axis=0)
        acc[h, 1] = jnp.dot(probs[...], grad, preferred_element_type=F32)

    after = {
        (0, 1): [(pass_on, 2, 3), (own_ahead, 3)],
        (0, 3): [(pass_on, 2, 2)],
        (1, 0): [(pass_on, 3, 3)],
        (1, 2): [(pass_on, 2, 1)],
        (1, 3): [(pass_on, 3, 2), (next_sum, 0, 1)],
        (2, 0): [(pass_on, 3, 1)],
        (2, 1): [(next_sum, 0, 2)],
        (2, 2): [(next_sum, 1, 1)],
        (2, 3): [(next_sum, 0, 3)],
        (3, 0): [(next_sum, 1, 2)],
        (3, 1): [(next_sum, 0, 4)],
        (3, 2): [(next_sum, 2, 1)],
        (3, 3): [(next_sum, 1, 3)],
    }
    for h in range(HEADS):
        wait_rows(h)
        wait_kv(h, 4)
        wait_kv(h, 0)
        prepare(h)
        for p in range(GROUP // 2):
            chunk(h, p)
            if p == GROUP // 2 - 1:
                key_sums(h)
                first_sum(h)
                start(out_remote(h))
                start(out_local(h))
            for event, *where in after.get((h, p), []):
                event(*where)
    for h, slot in ((2, 2), (3, 1), (1, 4), (2, 3), (3, 2), (2, 4), (3, 3), (3, 4)):
        next_sum(h, slot)

    for h in range(HEADS):
        for copy in own_to_ahead(h) + own_to_sibling(h) + rows_to_sibling(h):
            copy.wait_send()
        for slot in (3, 2, 1):
            forward(h, slot).wait_send()
        for slot in range(4):
            sum_copy(h, slot).wait_send()
        for copy in out_local(h) + fin_local(h):
            copy.wait()
        for copy in out_remote(h) + fin_remote(h):
            copy.wait_send()
        for part, dst in enumerate((att_out, dq_out)):
            ref = dst.at[:, head_cols(other, h, WIDE)]
            pltpu.make_async_copy(ref, ref, out_recv.at[h, part]).wait()
        for part, dst in enumerate((dk_out, dv_out)):
            ref = dst.at[:, head_cols(other, h, DH)]
            pltpu.make_async_copy(ref, ref, fin_recv.at[h, part]).wait()


def copy_out(*refs):
    sources, targets, sem = refs[:4], refs[4:8], refs[8]
    copies = []
    for src, dst in zip(sources, targets):
        pieces = 4 if src.shape[1] > 1024 else 1
        step = src.shape[0] // pieces
        for piece in range(pieces):
            rows = pl.ds(piece * step, step)
            copies.append(pltpu.make_async_copy(src.at[rows], dst.at[rows], sem.at[len(copies)]))
    for copy in copies:
        copy.start()
    for copy in copies:
        copy.wait()


def solution(mesh):
    devices = mesh.shape["cp"] * mesh.shape["hd"]
    anywhere = pl.BlockSpec(memory_space=pl.ANY)
    dma = pltpu.SemaphoreType.DMA

    def per_device(queries, key_vectors, value_vectors, out_grad, doc_lengths):
        wide = jax.ShapeDtypeStruct(queries.shape, BF16)
        narrow = jax.ShapeDtypeStruct(key_vectors.shape, BF16)
        results = pl.pallas_call(
            functools.partial(kernel, devices),
            out_shape=(wide, wide, narrow, narrow),
            in_specs=[anywhere] * 5,
            out_specs=(anywhere,) * 4,
            scratch_shapes=[
                pltpu.VMEM((HEADS, SLOTS, 2, CHIP, DH), BF16),
                pltpu.VMEM((HEADS, CHIP, WIDE), BF16),
                pltpu.VMEM((HEADS, CHIP, WIDE), BF16),
                pltpu.VMEM((HEADS, CHIP, WIDE), BF16),
                pltpu.VMEM((HEADS, CHIP, WIDE), BF16),
                pltpu.VMEM((HEADS, 2, KEYS, DH), F32),
                pltpu.VMEM((HEADS, 4, 2, CHIP, DH), BF16),
                pltpu.VMEM((HEADS, 4, 2, CHIP, DH), BF16),
                pltpu.VMEM((HEADS, 2, CHIP, DH), BF16),
                pltpu.VMEM((KEYS, DH), F32),
                pltpu.VMEM((1, 128), jnp.int32),
                pltpu.VMEM((KEYS, 2 * DH), BF16),
                pltpu.VMEM((DH, KEYS), BF16),
                pltpu.VMEM((KEYS, 2 * DH), BF16),
                pltpu.VMEM((DH + 16, KEYS), BF16),
                pltpu.VMEM((KEYS, PAIR), F32),
                pltpu.VMEM((KEYS, PAIR), BF16),
                pltpu.VMEM((KEYS, GROUP * CHIP), BF16),
                pltpu.VMEM((KEYS, GROUP * CHIP), BF16),
                dma,
                dma((HEADS, SLOTS)),
                dma((HEADS, 3)),
                dma((HEADS, 2, 2)),
                dma((HEADS, 2)),
                dma((HEADS, 2)),
                dma((HEADS, 2)),
                dma((HEADS, 4)),
                dma((HEADS, 4)),
                dma((HEADS, 2)),
                dma((HEADS, 2)),
                dma((HEADS, 2)),
                dma((HEADS, 2)),
                dma((HEADS, 2)),
                dma((HEADS, 2)),
            ],
            compiler_params=pltpu.CompilerParams(
                collective_id=0, has_side_effects=True, vmem_limit_bytes=56 * 1024 * 1024
            ),
            cost_estimate=pl.CostEstimate(
                flops=HEADS * GROUP * CHIP * KEYS * DH * 12,
                bytes_accessed=5 * 1024 * 1024,
                transcendentals=HEADS * GROUP * CHIP * KEYS,
            ),
        )(queries, key_vectors, value_vectors, out_grad, doc_lengths.reshape(1, -1))
        return pl.pallas_call(
            copy_out,
            out_shape=(wide, wide, narrow, narrow),
            in_specs=[pl.BlockSpec(memory_space=pltpu.HBM)] * 4,
            out_specs=(anywhere,) * 4,
            scratch_shapes=[dma((10,))],
        )(*results)

    token = P(("cp", "hd"), None)
    return jax.shard_map(
        per_device,
        mesh=mesh,
        in_specs=(token, token, token, token, P()),
        out_specs=(token,) * 4,
        check_vma=False,
    )
```

```python
import functools
import math

import jax
import jax.numpy as jnp
from jax import lax
from jax.experimental import pallas as pl
from jax.experimental.pallas import tpu as pltpu
from jax.sharding import PartitionSpec as P

DH = 128
ROWS = 64
CHIP = 2 * ROWS
SLOTS = 5
KEYS = SLOTS * CHIP
HEADS = 4
GROUP = 8
WIDE = GROUP * DH
PAIR = 2 * CHIP
SCALE = DH ** (-0.5)
MESH = pl.DeviceIdType.MESH
F32 = jnp.float32
BF16 = jnp.bfloat16


def kernel(
    devices,
    q_in, k_in, v_in, g_in, len_in,
    att_out, dq_out, dk_out, dv_out,
    kv, qb, gb, ob, dqb, acc, gin, gout, fin, bias, lens,
    key_pair, key_t, value_pair, value_t, scores, weights, probs, changes,
    k_own, v_own, q_away, g_away,
    len_sem, kv_recv, kv_fwd, own_ici, own_sib,
    qg_recv, qg_send, sum_recv, sum_send,
    out_send, out_recv, fin_send, fin_recv, kv_stage, qg_stage,
):
    cp = lax.axis_index("cp")
    hd = lax.axis_index("hd")
    me = cp * 8 + hd
    core = lax.rem(hd, 2)
    other = 1 - core

    def device(index):
        index = lax.rem(index + devices, devices)
        return (index // 8, lax.rem(index, 8))

    sibling = (cp, hd + 1 - 2 * core)
    chip_base = me - core
    ahead = device(me + 2)
    ahead_other = device(chip_base + 2 + other)
    behind = device(me - 2)
    behind_other = device(chip_base - 2 + other)
    my_rows = pl.ds(pl.multiple_of(core * ROWS, ROWS), ROWS)
    sib_rows = pl.ds(pl.multiple_of(other * ROWS, ROWS), ROWS)

    def head_cols(owner, h, width):
        return pl.ds(pl.multiple_of((owner * HEADS + h) * width, width), width)

    def remote(src, dst, send, recv, target):
        return pltpu.make_async_remote_copy(
            src_ref=src, dst_ref=dst, send_sem=send, recv_sem=recv, device_id=target, device_id_type=MESH
        )

    def own_to_ahead(h):
        made = []
        for side, (owner, target) in enumerate(((core, ahead), (other, ahead_other))):
            for part, src in enumerate((k_own, v_own)):
                made.append(remote(
                    src.at[:, head_cols(owner, h, DH)], kv.at[h, 3, part, my_rows],
                    own_ici.at[h, side, part], kv_recv.at[h, 3], target,
                ))
        return made

    def own_to_sibling(h):
        return [
            remote(src.at[:, head_cols(other, h, DH)], kv.at[h, 4, part, my_rows],
                   own_sib.at[h, part], kv_recv.at[h, 4], sibling)
            for part, src in enumerate((k_own, v_own))
        ]

    def own_local(h):
        return [
            pltpu.make_async_copy(src.at[:, head_cols(core, h, DH)], kv.at[h, 4, part, my_rows], kv_recv.at[h, 4])
            for part, src in enumerate((k_in, v_in))
        ]

    def rows_to_sibling(h):
        return [
            remote(src.at[h], dst.at[h, my_rows], qg_send.at[h, part], qg_recv.at[h, part], sibling)
            for part, (src, dst) in enumerate(((q_away, qb), (g_away, gb)))
        ]

    def stage_kv():
        return [
            pltpu.make_async_copy(src, dst, kv_stage.at[part])
            for part, (src, dst) in enumerate(((k_in, k_own), (v_in, v_own)))
        ]

    def stage_rows(h):
        return [
            pltpu.make_async_copy(src.at[:, head_cols(other, h, WIDE)], dst.at[h], qg_stage.at[h, part])
            for part, (src, dst) in enumerate(((q_in, q_away), (g_in, g_away)))
        ]

    def send_rows(h):
        for copy in stage_rows(h):
            copy.wait()
        start(rows_to_sibling(h))

    def rows_local(h):
        return [
            pltpu.make_async_copy(src.at[:, head_cols(core, h, WIDE)], dst.at[h, my_rows], qg_recv.at[h, part])
            for part, (src, dst) in enumerate(((q_in, qb), (g_in, gb)))
        ]

    def start(copies):
        for copy in copies:
            copy.start()

    def wait_kv(h, slot):
        pltpu.make_async_copy(kv.at[h, slot], kv.at[h, slot], kv_recv.at[h, slot]).wait()

    def wait_rows(h):
        for part, dst in enumerate((qb, gb)):
            pltpu.make_async_copy(dst.at[h], dst.at[h], qg_recv.at[h, part]).wait()

    def forward(h, slot):
        return remote(kv.at[h, slot], kv.at[h, slot - 1], kv_fwd.at[h, slot - 1], kv_recv.at[h, slot - 1], ahead)

    def own_ahead(h):
        start(own_to_ahead(h))

    def pass_on(h, slot):
        wait_kv(h, slot)
        forward(h, slot).start()

    def sum_copy(h, slot):
        return remote(gout.at[h, slot], gin.at[h, slot], sum_send.at[h, slot], sum_recv.at[h, slot], behind)

    def first_sum(h):
        for part in range(2):
            gout[h, 0, part] = acc[h, part, 0:CHIP].astype(BF16)
        sum_copy(h, 0).start()

    def next_sum(h, slot):
        pltpu.make_async_copy(gin.at[h, slot - 1], gin.at[h, slot - 1], sum_recv.at[h, slot - 1]).wait()
        for part in range(2):
            total = gin[h, slot - 1, part].astype(F32) + acc[h, part, slot * CHIP:(slot + 1) * CHIP]
            if slot < 4:
                gout[h, slot, part] = total.astype(BF16)
            else:
                fin[h, part] = total.astype(BF16)
        if slot < 4:
            sum_copy(h, slot).start()
        else:
            start(fin_remote(h))
            keep_fin(h)

    def keep_fin(h):
        for part, dst in enumerate((dk_out, dv_out)):
            dst[:, head_cols(core, h, DH)] = fin[h, part, my_rows]

    def fin_remote(h):
        return [
            remote(fin.at[h, part, sib_rows], dst.at[:, head_cols(core, h, DH)],
                   fin_send.at[h, part], fin_recv.at[h, part], sibling)
            for part, dst in enumerate((dk_out, dv_out))
        ]

    def keep_out(h):
        for src, dst in ((ob, att_out), (dqb, dq_out)):
            dst[:, head_cols(core, h, WIDE)] = src[h, my_rows]

    def out_remote(h):
        return [
            remote(src.at[h, sib_rows], dst.at[:, head_cols(core, h, WIDE)],
                   out_send.at[h, part], out_recv.at[h, part], sibling)
            for part, (src, dst) in enumerate(((ob, att_out), (dqb, dq_out)))
        ]

    barrier = pltpu.get_barrier_semaphore()
    for peer in (sibling, ahead, ahead_other, behind, behind_other):
        pl.semaphore_signal(barrier, inc=1, device_id=peer, device_id_type=MESH)
    len_copy = pltpu.make_async_copy(len_in, lens, len_sem)
    len_copy.start()
    start(stage_kv())
    for h in range(HEADS):
        start(own_local(h))
        start(stage_rows(h))
        start(rows_local(h))
    for copy in stage_kv():
        copy.wait()
    pl.semaphore_wait(barrier, 5)

    for h in range(3):
        own_ahead(h)
    for h in range(HEADS):
        start(own_to_sibling(h))
    send_rows(0)

    len_copy.wait()
    first_pos = (chip_base // 2) * CHIP
    low = lax.broadcasted_iota(jnp.int32, (DH, DH), 0)
    high = lax.broadcasted_iota(jnp.int32, (DH, DH), 1)
    ends_col = jnp.sum(jnp.where(high <= low, lens[...].astype(F32), 0.0), axis=1, keepdims=True)
    ends_row = jnp.sum(jnp.where(low == high, ends_col, 0.0), axis=0, keepdims=True)
    query_pos = high + first_pos
    query_seg = jnp.sum(jnp.where(ends_col <= query_pos.astype(F32), 1.0, 0.0), axis=0, keepdims=True)
    for slot in range(SLOTS):
        key_pos = low + (first_pos - (4 - slot) * CHIP)
        key_seg = jnp.sum(jnp.where(ends_row <= key_pos.astype(F32), 1.0, 0.0), axis=1, keepdims=True)
        allowed = (key_pos >= 0) & (key_pos <= query_pos) & (key_seg == query_seg)
        bias[slot * CHIP:(slot + 1) * CHIP, :] = jnp.where(allowed, 0.0, -1e30)

    pass_on(0, 3)
    own_ahead(3)
    send_rows(1)
    for h, slot in ((1, 3), (2, 3), (0, 2), (3, 3), (1, 2), (2, 2), (0, 1)):
        pass_on(h, slot)
    send_rows(2)
    for h, slot in ((3, 2), (1, 1), (2, 1)):
        pass_on(h, slot)
    send_rows(3)

    lane = lax.broadcasted_iota(jnp.int32, (PAIR, DH), 1)
    key_lane = lax.broadcasted_iota(jnp.int32, (KEYS, DH), 1)
    value_pair[:, DH:] = jnp.where(key_lane < 2, -1.0, 0.0).astype(BF16)
    value_t[DH:, :] = jnp.ones((16, KEYS), BF16)
    blocks = [slice(slot * CHIP, (slot + 1) * CHIP) for slot in range(SLOTS)]
    across = (((1,), (1,)), ((), ()))

    def prepare(h):
        keys = kv[h, :, 0].reshape(KEYS, DH)
        values = kv[h, :, 1].reshape(KEYS, DH)
        key_t[...] = keys.T
        value_t[:DH, :] = values.T
        value_pair[:, :DH] = values
        scaled = keys.astype(F32) * (SCALE * math.log2(math.e))
        scaled_top = scaled.astype(BF16)
        key_pair[:, :DH] = scaled_top
        key_pair[:, DH:] = (scaled - scaled_top.astype(F32)).astype(BF16)

    def chunk(h, p):
        cols = [slice((2 * p + i) * DH, (2 * p + i + 1) * DH) for i in range(2)]
        pair = slice(p * PAIR, (p + 1) * PAIR)
        query = jnp.concatenate([qb[h, :, c] for c in cols], axis=0)
        query = jnp.concatenate([query, query], axis=1)
        top = None
        for block in blocks:
            one_bias = bias[block]
            part = lax.dot_general(key_pair[block], query, across, preferred_element_type=F32)
            part = part + jnp.concatenate([one_bias, one_bias], axis=1)
            scores[block] = part
            part = jnp.max(part.reshape(CHIP // 8, 8, PAIR), axis=0)
            top = part if top is None else jnp.maximum(top, part)
        top = jnp.max(top, axis=0, keepdims=True)
        for block in blocks:
            weights[block] = jnp.exp2(scores[block] - top).astype(BF16)
        out = jnp.dot(value_t[...], weights[...], preferred_element_type=F32)
        inverse = 1.0 / out[DH:DH + 1]
        out = (out[:DH] * inverse).T.astype(BF16)
        grad = jnp.concatenate([gb[h, :, c] for c in cols], axis=0)
        for i, c in enumerate(cols):
            ob[h, :, c] = out[i * CHIP:(i + 1) * CHIP]
        delta = jnp.sum(out.astype(F32) * grad.astype(F32), axis=1, keepdims=True)
        delta_top = delta.astype(BF16).astype(F32)
        tail = jnp.where(lane == 0, delta_top, jnp.where(lane == 1, delta - delta_top, 0.0)).astype(BF16)
        grad = jnp.concatenate([grad, tail], axis=1)
        inverse = jnp.broadcast_to(inverse, (CHIP, PAIR)).astype(BF16)
        for block in blocks:
            change = lax.dot_general(value_pair[block], grad, across, preferred_element_type=F32).astype(BF16)
            prob = weights[block] * inverse
            probs[block, pair] = prob
            changes[block, pair] = prob * change
        query_grad = (jnp.dot(key_t[...], changes[:, pair], preferred_element_type=F32) * SCALE).T.astype(BF16)
        for i, c in enumerate(cols):
            dqb[h, :, c] = query_grad[i * CHIP:(i + 1) * CHIP]

    def key_sums(h):
        query = jnp.concatenate([qb[h, :, g * DH:(g + 1) * DH] for g in range(GROUP)], axis=0)
        acc[h, 0] = jnp.dot(changes[...], query, preferred_element_type=F32) * SCALE
        grad = jnp.concatenate([gb[h, :, g * DH:(g + 1) * DH] for g in range(GROUP)], axis=0)
        acc[h, 1] = jnp.dot(probs[...], grad, preferred_element_type=F32)

    after = {
        (0, 0): [(pass_on, 3, 1)],
        (1, 2): [(next_sum, 0, 1)],
        (2, 1): [(next_sum, 0, 2)],
        (2, 2): [(next_sum, 1, 1)],
        (3, 0): [(next_sum, 0, 3)],
        (3, 1): [(next_sum, 1, 2)],
        (3, 2): [(next_sum, 2, 1)],
        (3, 3): [(next_sum, 0, 4), (next_sum, 1, 3)],
    }
    for h in range(HEADS):
        wait_rows(h)
        wait_kv(h, 4)
        wait_kv(h, 0)
        prepare(h)
        for p in range(GROUP // 2):
            chunk(h, p)
            if p == GROUP // 2 - 1:
                key_sums(h)
                first_sum(h)
                start(out_remote(h))
                keep_out(h)
            for event, *where in after.get((h, p), []):
                event(*where)
    for h, slot in ((2, 2), (3, 1), (1, 4), (2, 3), (3, 2), (2, 4), (3, 3), (3, 4)):
        next_sum(h, slot)

    for h in range(HEADS):
        for copy in own_to_ahead(h) + own_to_sibling(h) + rows_to_sibling(h):
            copy.wait_send()
        for slot in (3, 2, 1):
            forward(h, slot).wait_send()
        for slot in range(4):
            sum_copy(h, slot).wait_send()
        for copy in out_remote(h) + fin_remote(h):
            copy.wait_send()
        for part, dst in enumerate((att_out, dq_out)):
            ref = dst.at[:, head_cols(other, h, WIDE)]
            pltpu.make_async_copy(ref, ref, out_recv.at[h, part]).wait()
        for part, dst in enumerate((dk_out, dv_out)):
            ref = dst.at[:, head_cols(other, h, DH)]
            pltpu.make_async_copy(ref, ref, fin_recv.at[h, part]).wait()


def copy_out(*refs):
    sources, targets, sem = refs[:4], refs[4:8], refs[8]
    copies = []
    for src, dst in zip(sources, targets):
        pieces = 4 if src.shape[1] > 1024 else 1
        step = src.shape[0] // pieces
        for piece in range(pieces):
            rows = pl.ds(piece * step, step)
            copies.append(pltpu.make_async_copy(src.at[rows], dst.at[rows], sem.at[len(copies)]))
    for copy in copies:
        copy.start()
    for copy in copies:
        copy.wait()


def solution(mesh):
    devices = mesh.shape["cp"] * mesh.shape["hd"]
    anywhere = pl.BlockSpec(memory_space=pl.ANY)
    dma = pltpu.SemaphoreType.DMA

    def per_device(queries, key_vectors, value_vectors, out_grad, doc_lengths):
        wide = jax.ShapeDtypeStruct(queries.shape, BF16)
        narrow = jax.ShapeDtypeStruct(key_vectors.shape, BF16)
        results = pl.pallas_call(
            functools.partial(kernel, devices),
            out_shape=tuple(pltpu.VMEM(x.shape, BF16) for x in (wide, wide, narrow, narrow)),
            in_specs=[anywhere] * 5,
            out_specs=(pl.BlockSpec(memory_space=pltpu.VMEM),) * 4,
            scratch_shapes=[
                pltpu.VMEM((HEADS, SLOTS, 2, CHIP, DH), BF16),
                pltpu.VMEM((HEADS, CHIP, WIDE), BF16),
                pltpu.VMEM((HEADS, CHIP, WIDE), BF16),
                pltpu.VMEM((HEADS, CHIP, WIDE), BF16),
                pltpu.VMEM((HEADS, CHIP, WIDE), BF16),
                pltpu.VMEM((HEADS, 2, KEYS, DH), F32),
                pltpu.VMEM((HEADS, 4, 2, CHIP, DH), BF16),
                pltpu.VMEM((HEADS, 4, 2, CHIP, DH), BF16),
                pltpu.VMEM((HEADS, 2, CHIP, DH), BF16),
                pltpu.VMEM((KEYS, DH), F32),
                pltpu.VMEM((1, 128), jnp.int32),
                pltpu.VMEM((KEYS, 2 * DH), BF16),
                pltpu.VMEM((DH, KEYS), BF16),
                pltpu.VMEM((KEYS, 2 * DH), BF16),
                pltpu.VMEM((DH + 16, KEYS), BF16),
                pltpu.VMEM((KEYS, PAIR), F32),
                pltpu.VMEM((KEYS, PAIR), BF16),
                pltpu.VMEM((KEYS, GROUP * CHIP), BF16),
                pltpu.VMEM((KEYS, GROUP * CHIP), BF16),
                pltpu.VMEM((ROWS, 2 * HEADS * DH), BF16),
                pltpu.VMEM((ROWS, 2 * HEADS * DH), BF16),
                pltpu.VMEM((HEADS, ROWS, WIDE), BF16),
                pltpu.VMEM((HEADS, ROWS, WIDE), BF16),
                dma,
                dma((HEADS, SLOTS)),
                dma((HEADS, 3)),
                dma((HEADS, 2, 2)),
                dma((HEADS, 2)),
                dma((HEADS, 2)),
                dma((HEADS, 2)),
                dma((HEADS, 4)),
                dma((HEADS, 4)),
                dma((HEADS, 2)),
                dma((HEADS, 2)),
                dma((HEADS, 2)),
                dma((HEADS, 2)),
                dma((2,)),
                dma((HEADS, 2)),
            ],
            compiler_params=pltpu.CompilerParams(
                collective_id=0, has_side_effects=True, vmem_limit_bytes=56 * 1024 * 1024
            ),
            cost_estimate=pl.CostEstimate(
                flops=HEADS * GROUP * CHIP * KEYS * DH * 12,
                bytes_accessed=5 * 1024 * 1024,
                transcendentals=HEADS * GROUP * CHIP * KEYS,
            ),
        )(queries, key_vectors, value_vectors, out_grad, doc_lengths.reshape(1, -1))
        return pl.pallas_call(
            copy_out,
            out_shape=(wide, wide, narrow, narrow),
            in_specs=[pl.BlockSpec(memory_space=pltpu.VMEM)] * 4,
            out_specs=(anywhere,) * 4,
            scratch_shapes=[dma((10,))],
            compiler_params=pltpu.CompilerParams(vmem_limit_bytes=8 * 1024 * 1024),
        )(*results)

    token = P(("cp", "hd"), None)
    return jax.shard_map(
        per_device,
        mesh=mesh,
        in_specs=(token, token, token, token, P()),
        out_specs=(token,) * 4,
        check_vma=False,
    )
```

```python
import functools
import math

import jax
import jax.numpy as jnp
from jax import lax
from jax.experimental import pallas as pl
from jax.experimental.pallas import tpu as pltpu
from jax.sharding import PartitionSpec as P

DH = 128
ROWS = 64
CHIP = 2 * ROWS
SLOTS = 5
KEYS = SLOTS * CHIP
HEADS = 4
GROUP = 8
WIDE = GROUP * DH
PAIR = 2 * CHIP
CHUNKS = GROUP // 2
SCALE = DH ** (-0.5)
MESH = pl.DeviceIdType.MESH
F32 = jnp.float32
BF16 = jnp.bfloat16


def kernel(
    devices,
    q_in, k_in, v_in, g_in, len_in,
    att_out, dq_out, dk_out, dv_out,
    kv, qb, gb, ob, dqb, acc, gin, gout, fin, bias, lens,
    key_t, value_t, grad_t, scores, tops, rows, weights, probs, changes,
    k_own, v_own, q_away, g_away,
    len_sem, kv_recv, kv_fwd, own_ici, own_sib,
    qg_recv, qg_send, sum_recv, sum_send,
    out_send, out_recv, fin_send, fin_recv, kv_stage, qg_stage,
):
    cp = lax.axis_index("cp")
    hd = lax.axis_index("hd")
    me = cp * 8 + hd
    core = lax.rem(hd, 2)
    other = 1 - core

    def device(index):
        index = lax.rem(index + devices, devices)
        return (index // 8, lax.rem(index, 8))

    sibling = (cp, hd + 1 - 2 * core)
    chip_base = me - core
    ahead = device(me + 2)
    ahead_other = device(chip_base + 2 + other)
    behind = device(me - 2)
    behind_other = device(chip_base - 2 + other)
    my_rows = pl.ds(pl.multiple_of(core * ROWS, ROWS), ROWS)
    sib_rows = pl.ds(pl.multiple_of(other * ROWS, ROWS), ROWS)

    def head_cols(owner, h, width):
        return pl.ds(pl.multiple_of((owner * HEADS + h) * width, width), width)

    def remote(src, dst, send, recv, target):
        return pltpu.make_async_remote_copy(
            src_ref=src, dst_ref=dst, send_sem=send, recv_sem=recv, device_id=target, device_id_type=MESH
        )

    def own_to_ahead(h):
        made = []
        for side, (owner, target) in enumerate(((core, ahead), (other, ahead_other))):
            for part, src in enumerate((k_own, v_own)):
                made.append(remote(
                    src.at[:, head_cols(owner, h, DH)], kv.at[h, 3, part, my_rows],
                    own_ici.at[h, side, part], kv_recv.at[h, 3], target,
                ))
        return made

    def own_to_sibling(h):
        return [
            remote(src.at[:, head_cols(other, h, DH)], kv.at[h, 4, part, my_rows],
                   own_sib.at[h, part], kv_recv.at[h, 4], sibling)
            for part, src in enumerate((k_own, v_own))
        ]

    def own_local(h):
        return [
            pltpu.make_async_copy(src.at[:, head_cols(core, h, DH)], kv.at[h, 4, part, my_rows], kv_recv.at[h, 4])
            for part, src in enumerate((k_in, v_in))
        ]

    def rows_to_sibling(h):
        return [
            remote(src.at[h], dst.at[h, my_rows], qg_send.at[h, part], qg_recv.at[h, part], sibling)
            for part, (src, dst) in enumerate(((q_away, qb), (g_away, gb)))
        ]

    def stage_kv():
        return [
            pltpu.make_async_copy(src, dst, kv_stage.at[part])
            for part, (src, dst) in enumerate(((k_in, k_own), (v_in, v_own)))
        ]

    def stage_rows(h):
        return [
            pltpu.make_async_copy(src.at[:, head_cols(other, h, WIDE)], dst.at[h], qg_stage.at[h, part])
            for part, (src, dst) in enumerate(((q_in, q_away), (g_in, g_away)))
        ]

    def send_rows(h):
        for copy in stage_rows(h):
            copy.wait()
        start(rows_to_sibling(h))

    def rows_local(h):
        return [
            pltpu.make_async_copy(src.at[:, head_cols(core, h, WIDE)], dst.at[h, my_rows], qg_recv.at[h, part])
            for part, (src, dst) in enumerate(((q_in, qb), (g_in, gb)))
        ]

    def start(copies):
        for copy in copies:
            copy.start()

    def wait_kv(h, slot):
        pltpu.make_async_copy(kv.at[h, slot], kv.at[h, slot], kv_recv.at[h, slot]).wait()

    def wait_rows(h):
        for part, dst in enumerate((qb, gb)):
            pltpu.make_async_copy(dst.at[h], dst.at[h], qg_recv.at[h, part]).wait()

    def forward(h, slot):
        return remote(kv.at[h, slot], kv.at[h, slot - 1], kv_fwd.at[h, slot - 1], kv_recv.at[h, slot - 1], ahead)

    def own_ahead(h):
        start(own_to_ahead(h))

    def pass_on(h, slot):
        wait_kv(h, slot)
        forward(h, slot).start()

    def sum_copy(h, slot):
        return remote(gout.at[h, slot], gin.at[h, slot], sum_send.at[h, slot], sum_recv.at[h, slot], behind)

    def first_sum(h):
        for part in range(2):
            gout[h, 0, part] = (acc[h, part, 0:CHIP] * (SCALE, 1.0)[part]).astype(BF16)
        sum_copy(h, 0).start()

    def next_sum(h, slot):
        pltpu.make_async_copy(gin.at[h, slot - 1], gin.at[h, slot - 1], sum_recv.at[h, slot - 1]).wait()
        for part in range(2):
            mine = acc[h, part, slot * CHIP:(slot + 1) * CHIP] * (SCALE, 1.0)[part]
            total = gin[h, slot - 1, part].astype(F32) + mine
            if slot < 4:
                gout[h, slot, part] = total.astype(BF16)
            else:
                fin[h, part] = total.astype(BF16)
        if slot < 4:
            sum_copy(h, slot).start()
        else:
            start(fin_remote(h))
            keep_fin(h)

    def keep_fin(h):
        for part, dst in enumerate((dk_out, dv_out)):
            dst[:, head_cols(core, h, DH)] = fin[h, part, my_rows]

    def fin_remote(h):
        return [
            remote(fin.at[h, part, sib_rows], dst.at[:, head_cols(core, h, DH)],
                   fin_send.at[h, part], fin_recv.at[h, part], sibling)
            for part, dst in enumerate((dk_out, dv_out))
        ]

    def keep_out(h):
        for src, dst in ((ob, att_out), (dqb, dq_out)):
            dst[:, head_cols(core, h, WIDE)] = src[h, my_rows]

    def out_remote(h):
        return [
            remote(src.at[h, sib_rows], dst.at[:, head_cols(core, h, WIDE)],
                   out_send.at[h, part], out_recv.at[h, part], sibling)
            for part, (src, dst) in enumerate(((ob, att_out), (dqb, dq_out)))
        ]

    barrier = pltpu.get_barrier_semaphore()
    for peer in (sibling, ahead, ahead_other, behind, behind_other):
        pl.semaphore_signal(barrier, inc=1, device_id=peer, device_id_type=MESH)
    len_copy = pltpu.make_async_copy(len_in, lens, len_sem)
    len_copy.start()
    start(stage_kv())
    for h in range(HEADS):
        start(own_local(h))
        start(stage_rows(h))
        start(rows_local(h))
    for copy in stage_kv():
        copy.wait()
    pl.semaphore_wait(barrier, 5)

    for h in range(2):
        own_ahead(h)
    for h in range(HEADS):
        start(own_to_sibling(h))
    send_rows(0)

    len_copy.wait()
    first_pos = (chip_base // 2) * CHIP
    low = lax.broadcasted_iota(jnp.int32, (DH, DH), 0)
    high = lax.broadcasted_iota(jnp.int32, (DH, DH), 1)
    ends_col = jnp.sum(jnp.where(high <= low, lens[...].astype(F32), 0.0), axis=1, keepdims=True)
    ends_row = jnp.sum(jnp.where(low == high, ends_col, 0.0), axis=0, keepdims=True)
    query_pos = high + first_pos
    query_seg = jnp.sum(jnp.where(ends_col <= query_pos.astype(F32), 1.0, 0.0), axis=0, keepdims=True)
    for slot in range(SLOTS):
        key_pos = low + (first_pos - (4 - slot) * CHIP)
        key_seg = jnp.sum(jnp.where(ends_row <= key_pos.astype(F32), 1.0, 0.0), axis=1, keepdims=True)
        allowed = (key_pos >= 0) & (key_pos <= query_pos) & (key_seg == query_seg)
        bias[slot * CHIP:(slot + 1) * CHIP, :] = jnp.where(allowed, 0.0, -1e30)

    pass_on(0, 3)
    own_ahead(2)
    send_rows(1)
    for h, slot in ((1, 3), (0, 2), (2, 3), (1, 2), (0, 1)):
        pass_on(h, slot)
    own_ahead(3)
    send_rows(2)
    pass_on(2, 2)
    pass_on(1, 1)
    send_rows(3)

    for side in range(2):
        value_t[side, DH:, :] = jnp.ones((16, KEYS), BF16)
    blocks = [slice(slot * CHIP, (slot + 1) * CHIP) for slot in range(SLOTS)]

    def cols_of(c):
        first = 2 * (c % CHUNKS)
        return [slice((first + i) * DH, (first + i + 1) * DH) for i in range(2)]

    def prepare(h):
        key_t[h % 2] = kv[h, :, 0].reshape(KEYS, DH).T
        value_t[h % 2, :DH, :] = kv[h, :, 1].reshape(KEYS, DH).T

    def score_stage(c):
        h, side = c // CHUNKS, c % 2
        query = jnp.concatenate([qb[h, :, col].T for col in cols_of(c)], axis=1)
        raw = jnp.dot(kv[h, :, 0].reshape(KEYS, DH), query, preferred_element_type=F32)
        top = None
        for block in blocks:
            one_bias = bias[block]
            part = raw[block] * (SCALE * math.log2(math.e)) + jnp.concatenate([one_bias, one_bias], axis=1)
            scores[side, block] = part
            part = jnp.max(part.reshape(CHIP // 8, 8, PAIR), axis=0)
            top = part if top is None else jnp.maximum(top, part)
        tops[side] = top

    def out_stage(c):
        h, side = c // CHUNKS, c % 2
        top = jnp.max(tops[side], axis=0, keepdims=True)
        for block in blocks:
            weights[side, block] = jnp.exp2(scores[side, block] - top).astype(BF16)
        out = jnp.dot(value_t[h % 2], weights[side], preferred_element_type=F32)
        inverse = 1.0 / out[DH:DH + 1]
        out = out[:DH] * inverse
        cols = cols_of(c)
        grad = jnp.concatenate([gb[h, :, col].T for col in cols], axis=1)
        grad_t[side] = grad
        delta = jnp.sum(out.astype(BF16).astype(F32) * grad.astype(F32), axis=0, keepdims=True)
        rows[side, 0] = jnp.broadcast_to(inverse, (8, PAIR))
        rows[side, 1] = jnp.broadcast_to(delta, (8, PAIR))
        out = out.T.astype(BF16)
        for i, col in enumerate(cols):
            ob[h, :, col] = out[i * CHIP:(i + 1) * CHIP]

    def change_stage(c):
        h, side = c // CHUNKS, c % 2
        raw = jnp.dot(kv[h, :, 1].reshape(KEYS, DH), grad_t[side], preferred_element_type=F32)
        inverse = jnp.broadcast_to(rows[side, 0, 0:1], (CHIP, PAIR)).astype(BF16)
        delta = rows[side, 1, 0:1]
        for block in blocks:
            prob = weights[side, block] * inverse
            probs[side, block] = prob
            changes[side, block] = prob * (raw[block] - delta).astype(BF16)

    def grad_stage(c):
        h, side = c // CHUNKS, c % 2
        cols = cols_of(c)
        query_grad = (jnp.dot(key_t[h % 2], changes[side], preferred_element_type=F32) * SCALE).T.astype(BF16)
        for i, col in enumerate(cols):
            dqb[h, :, col] = query_grad[i * CHIP:(i + 1) * CHIP]
        for part, (left, right) in enumerate(((changes, qb), (probs, gb))):
            right = jnp.concatenate([right[h, :, col] for col in cols], axis=0)
            total = jnp.dot(left[side], right, preferred_element_type=F32)
            if c % CHUNKS == 0:
                acc[h, part] = total
            else:
                acc[h, part] += total

    after = {
        0: [(pass_on, 3, 3)],
        1: [(pass_on, 2, 1)],
        3: [(pass_on, 3, 2)],
        6: [(pass_on, 3, 1)],
        9: [(next_sum, 0, 1)],
        12: [(next_sum, 0, 2)],
        13: [(next_sum, 1, 1)],
        15: [(next_sum, 0, 3)],
        16: [(next_sum, 1, 2)],
        17: [(next_sum, 2, 1)],
        18: [(next_sum, 0, 4)],
    }
    steps = HEADS * CHUNKS
    for step in range(steps + 3):
        if step < steps and step % CHUNKS == 0:
            h = step // CHUNKS
            wait_rows(h)
            wait_kv(h, 4)
            wait_kv(h, 0)
            prepare(h)
        if step < steps:
            score_stage(step)
        if 0 <= step - 2 < steps:
            change_stage(step - 2)
        if 0 <= step - 1 < steps:
            out_stage(step - 1)
        if 0 <= step - 3:
            grad_stage(step - 3)
            if (step - 3) % CHUNKS == CHUNKS - 1:
                h = (step - 3) // CHUNKS
                first_sum(h)
                start(out_remote(h))
                keep_out(h)
        for event, *where in after.get(step, []):
            event(*where)
    for h, slot in ((1, 3), (2, 2), (3, 1), (1, 4), (2, 3), (3, 2), (2, 4), (3, 3), (3, 4)):
        next_sum(h, slot)

    for h in range(HEADS):
        for copy in own_to_ahead(h) + own_to_sibling(h) + rows_to_sibling(h):
            copy.wait_send()
        for slot in (3, 2, 1):
            forward(h, slot).wait_send()
        for slot in range(4):
            sum_copy(h, slot).wait_send()
        for copy in out_remote(h) + fin_remote(h):
            copy.wait_send()
        for part, dst in enumerate((att_out, dq_out)):
            ref = dst.at[:, head_cols(other, h, WIDE)]
            pltpu.make_async_copy(ref, ref, out_recv.at[h, part]).wait()
        for part, dst in enumerate((dk_out, dv_out)):
            ref = dst.at[:, head_cols(other, h, DH)]
            pltpu.make_async_copy(ref, ref, fin_recv.at[h, part]).wait()


def copy_out(*refs):
    sources, targets, sem = refs[:4], refs[4:8], refs[8]
    copies = []
    for src, dst in zip(sources, targets):
        pieces = 4 if src.shape[1] > 1024 else 1
        step = src.shape[0] // pieces
        for piece in range(pieces):
            rows = pl.ds(piece * step, step)
            copies.append(pltpu.make_async_copy(src.at[rows], dst.at[rows], sem.at[len(copies)]))
    for copy in copies:
        copy.start()
    for copy in copies:
        copy.wait()


def solution(mesh):
    devices = mesh.shape["cp"] * mesh.shape["hd"]
    anywhere = pl.BlockSpec(memory_space=pl.ANY)
    dma = pltpu.SemaphoreType.DMA

    def per_device(queries, key_vectors, value_vectors, out_grad, doc_lengths):
        wide = jax.ShapeDtypeStruct(queries.shape, BF16)
        narrow = jax.ShapeDtypeStruct(key_vectors.shape, BF16)
        results = pl.pallas_call(
            functools.partial(kernel, devices),
            out_shape=tuple(pltpu.VMEM(x.shape, BF16) for x in (wide, wide, narrow, narrow)),
            in_specs=[anywhere] * 5,
            out_specs=(pl.BlockSpec(memory_space=pltpu.VMEM),) * 4,
            scratch_shapes=[
                pltpu.VMEM((HEADS, SLOTS, 2, CHIP, DH), BF16),
                pltpu.VMEM((HEADS, CHIP, WIDE), BF16),
                pltpu.VMEM((HEADS, CHIP, WIDE), BF16),
                pltpu.VMEM((HEADS, CHIP, WIDE), BF16),
                pltpu.VMEM((HEADS, CHIP, WIDE), BF16),
                pltpu.VMEM((HEADS, 2, KEYS, DH), F32),
                pltpu.VMEM((HEADS, 4, 2, CHIP, DH), BF16),
                pltpu.VMEM((HEADS, 4, 2, CHIP, DH), BF16),
                pltpu.VMEM((HEADS, 2, CHIP, DH), BF16),
                pltpu.VMEM((KEYS, DH), F32),
                pltpu.VMEM((1, 128), jnp.int32),
                pltpu.VMEM((2, DH, KEYS), BF16),
                pltpu.VMEM((2, DH + 16, KEYS), BF16),
                pltpu.VMEM((2, DH, PAIR), BF16),
                pltpu.VMEM((2, KEYS, PAIR), F32),
                pltpu.VMEM((2, 8, PAIR), F32),
                pltpu.VMEM((2, 2, 8, PAIR), F32),
                pltpu.VMEM((2, KEYS, PAIR), BF16),
                pltpu.VMEM((2, KEYS, PAIR), BF16),
                pltpu.VMEM((2, KEYS, PAIR), BF16),
                pltpu.VMEM((ROWS, 2 * HEADS * DH), BF16),
                pltpu.VMEM((ROWS, 2 * HEADS * DH), BF16),
                pltpu.VMEM((HEADS, ROWS, WIDE), BF16),
                pltpu.VMEM((HEADS, ROWS, WIDE), BF16),
                dma,
                dma((HEADS, SLOTS)),
                dma((HEADS, 3)),
                dma((HEADS, 2, 2)),
                dma((HEADS, 2)),
                dma((HEADS, 2)),
                dma((HEADS, 2)),
                dma((HEADS, 4)),
                dma((HEADS, 4)),
                dma((HEADS, 2)),
                dma((HEADS, 2)),
                dma((HEADS, 2)),
                dma((HEADS, 2)),
                dma((2,)),
                dma((HEADS, 2)),
            ],
            compiler_params=pltpu.CompilerParams(
                collective_id=0, has_side_effects=True, vmem_limit_bytes=56 * 1024 * 1024
            ),
            cost_estimate=pl.CostEstimate(
                flops=HEADS * GROUP * CHIP * KEYS * DH * 12,
                bytes_accessed=5 * 1024 * 1024,
                transcendentals=HEADS * GROUP * CHIP * KEYS,
            ),
        )(queries, key_vectors, value_vectors, out_grad, doc_lengths.reshape(1, -1))
        return pl.pallas_call(
            copy_out,
            out_shape=(wide, wide, narrow, narrow),
            in_specs=[pl.BlockSpec(memory_space=pltpu.VMEM)] * 4,
            out_specs=(anywhere,) * 4,
            scratch_shapes=[dma((10,))],
            compiler_params=pltpu.CompilerParams(vmem_limit_bytes=8 * 1024 * 1024),
        )(*results)

    token = P(("cp", "hd"), None)
    return jax.shard_map(
        per_device,
        mesh=mesh,
        in_specs=(token, token, token, token, P()),
        out_specs=(token,) * 4,
        check_vma=False,
    )
```

```python
import functools
import math

import jax
import jax.numpy as jnp
from jax import lax
from jax.experimental import pallas as pl
from jax.experimental.pallas import tpu as pltpu
from jax.sharding import PartitionSpec as P

DH = 128
ROWS = 64
CHIP = 2 * ROWS
SLOTS = 5
KEYS = SLOTS * CHIP
HEADS = 4
GROUP = 8
WIDE = GROUP * DH
PAIR = 2 * CHIP
CHUNKS = GROUP // 2
SCALE = DH ** (-0.5)
MESH = pl.DeviceIdType.MESH
F32 = jnp.float32
BF16 = jnp.bfloat16


def kernel(
    devices,
    q_in, k_in, v_in, g_in, len_in,
    att_out, dq_out, dk_out, dv_out,
    kv, qb, gb, ob, dqb, acc, gin, gout, fin, bias, lens,
    key_t, value_t, grad_t, scores, tops, rows, weights, probs, changes,
    k_own, v_own, q_away, g_away,
    len_sem, kv_recv, kv_fwd, own_ici, own_sib,
    qg_recv, qg_send, sum_recv, sum_send,
    out_send, out_recv, fin_send, fin_recv, kv_stage, qg_stage,
):
    cp = lax.axis_index("cp")
    hd = lax.axis_index("hd")
    me = cp * 8 + hd
    core = lax.rem(hd, 2)
    other = 1 - core

    def device(index):
        index = lax.rem(index + devices, devices)
        return (index // 8, lax.rem(index, 8))

    sibling = (cp, hd + 1 - 2 * core)
    chip_base = me - core
    ahead = device(me + 2)
    ahead_other = device(chip_base + 2 + other)
    behind = device(me - 2)
    behind_other = device(chip_base - 2 + other)
    my_rows = pl.ds(pl.multiple_of(core * ROWS, ROWS), ROWS)
    sib_rows = pl.ds(pl.multiple_of(other * ROWS, ROWS), ROWS)

    def head_cols(owner, h, width):
        return pl.ds(pl.multiple_of((owner * HEADS + h) * width, width), width)

    def remote(src, dst, send, recv, target):
        return pltpu.make_async_remote_copy(
            src_ref=src, dst_ref=dst, send_sem=send, recv_sem=recv, device_id=target, device_id_type=MESH
        )

    def own_to_ahead(h):
        made = []
        for side, (owner, target) in enumerate(((core, ahead), (other, ahead_other))):
            for part, src in enumerate((k_own, v_own)):
                made.append(remote(
                    src.at[:, head_cols(owner, h, DH)], kv.at[h, 3, part, my_rows],
                    own_ici.at[h, side, part], kv_recv.at[h, 3, part], target,
                ))
        return made

    def own_to_sibling(h):
        return [
            remote(src.at[:, head_cols(other, h, DH)], kv.at[h, 4, part, my_rows],
                   own_sib.at[h, part], kv_recv.at[h, 4, part], sibling)
            for part, src in enumerate((k_own, v_own))
        ]

    def own_local(h):
        return [
            pltpu.make_async_copy(src.at[:, head_cols(core, h, DH)], kv.at[h, 4, part, my_rows], kv_recv.at[h, 4, part])
            for part, src in enumerate((k_in, v_in))
        ]

    def rows_to_sibling(h):
        return [
            remote(src.at[h], dst.at[h, my_rows], qg_send.at[h, part], qg_recv.at[h, part], sibling)
            for part, (src, dst) in enumerate(((q_away, qb), (g_away, gb)))
        ]

    def stage_kv():
        return [
            pltpu.make_async_copy(src, dst, kv_stage.at[part])
            for part, (src, dst) in enumerate(((k_in, k_own), (v_in, v_own)))
        ]

    def stage_rows(h):
        return [
            pltpu.make_async_copy(src.at[:, head_cols(other, h, WIDE)], dst.at[h], qg_stage.at[h, part])
            for part, (src, dst) in enumerate(((q_in, q_away), (g_in, g_away)))
        ]

    def send_rows(h):
        for copy in stage_rows(h):
            copy.wait()
        start(rows_to_sibling(h))

    def rows_local(h):
        return [
            pltpu.make_async_copy(src.at[:, head_cols(core, h, WIDE)], dst.at[h, my_rows], qg_recv.at[h, part])
            for part, (src, dst) in enumerate(((q_in, qb), (g_in, gb)))
        ]

    def start(copies):
        for copy in copies:
            copy.start()

    def wait_kv(h, slot, part):
        ref = kv.at[h, slot, part]
        pltpu.make_async_copy(ref, ref, kv_recv.at[h, slot, part]).wait()

    def wait_rows(h):
        for part, dst in enumerate((qb, gb)):
            pltpu.make_async_copy(dst.at[h], dst.at[h], qg_recv.at[h, part]).wait()

    def forward(h, slot, part):
        return remote(kv.at[h, slot, part], kv.at[h, slot - 1, part],
                      kv_fwd.at[h, slot - 1, part], kv_recv.at[h, slot - 1, part], ahead)

    def own_ahead(h):
        start(own_to_ahead(h))

    def pass_on(h, slot):
        for part in range(2):
            wait_kv(h, slot, part)
            forward(h, slot, part).start()

    def sum_copy(h, slot, part):
        return remote(gout.at[h, slot, part], gin.at[h, slot, part],
                      sum_send.at[h, slot, part], sum_recv.at[h, slot, part], behind)

    def first_sum(h):
        for part in range(2):
            gout[h, 0, part] = (acc[h, part, 0:CHIP] * (SCALE, 1.0)[part]).astype(BF16)
            sum_copy(h, 0, part).start()

    def next_sum(h, slot):
        for part in range(2):
            ref = gin.at[h, slot - 1, part]
            pltpu.make_async_copy(ref, ref, sum_recv.at[h, slot - 1, part]).wait()
            mine = acc[h, part, slot * CHIP:(slot + 1) * CHIP] * (SCALE, 1.0)[part]
            total = gin[h, slot - 1, part].astype(F32) + mine
            if slot < 4:
                gout[h, slot, part] = total.astype(BF16)
                sum_copy(h, slot, part).start()
            else:
                fin[h, part] = total.astype(BF16)
                fin_remote(h, part).start()
        if slot == 4:
            keep_fin(h)

    def keep_fin(h):
        for part, dst in enumerate((dk_out, dv_out)):
            dst[:, head_cols(core, h, DH)] = fin[h, part, my_rows]

    def fin_remote(h, part):
        return remote(fin.at[h, part, sib_rows], (dk_out, dv_out)[part].at[:, head_cols(core, h, DH)],
                      fin_send.at[h, part], fin_recv.at[h, part], sibling)

    def keep_out(h):
        for src, dst in ((ob, att_out), (dqb, dq_out)):
            dst[:, head_cols(core, h, WIDE)] = src[h, my_rows]

    def out_remote(h):
        return [
            remote(src.at[h, sib_rows], dst.at[:, head_cols(core, h, WIDE)],
                   out_send.at[h, part], out_recv.at[h, part], sibling)
            for part, (src, dst) in enumerate(((ob, att_out), (dqb, dq_out)))
        ]

    barrier = pltpu.get_barrier_semaphore()
    for peer in (sibling, ahead, ahead_other, behind, behind_other):
        pl.semaphore_signal(barrier, inc=1, device_id=peer, device_id_type=MESH)
    len_copy = pltpu.make_async_copy(len_in, lens, len_sem)
    len_copy.start()
    start(stage_kv())
    for h in range(HEADS):
        start(own_local(h))
        start(stage_rows(h))
        start(rows_local(h))
    for copy in stage_kv():
        copy.wait()
    pl.semaphore_wait(barrier, 5)

    own_ahead(0)
    start(own_to_sibling(0))
    send_rows(0)
    for h in range(1, HEADS):
        start(own_to_sibling(h))

    len_copy.wait()
    first_pos = (chip_base // 2) * CHIP
    low = lax.broadcasted_iota(jnp.int32, (DH, DH), 0)
    high = lax.broadcasted_iota(jnp.int32, (DH, DH), 1)
    ends_col = jnp.sum(jnp.where(high <= low, lens[...].astype(F32), 0.0), axis=1, keepdims=True)
    ends_row = jnp.sum(jnp.where(low == high, ends_col, 0.0), axis=0, keepdims=True)
    query_pos = high + first_pos
    query_seg = jnp.sum(jnp.where(ends_col <= query_pos.astype(F32), 1.0, 0.0), axis=0, keepdims=True)
    for slot in range(SLOTS):
        key_pos = low + (first_pos - (4 - slot) * CHIP)
        key_seg = jnp.sum(jnp.where(ends_row <= key_pos.astype(F32), 1.0, 0.0), axis=1, keepdims=True)
        allowed = (key_pos >= 0) & (key_pos <= query_pos) & (key_seg == query_seg)
        bias[slot * CHIP:(slot + 1) * CHIP, :] = jnp.where(allowed, 0.0, -1e30)

    pass_on(0, 3)
    pass_on(0, 2)
    own_ahead(1)
    pass_on(0, 1)
    send_rows(1)
    pass_on(1, 3)

    for side in range(2):
        value_t[side, DH:, :] = jnp.ones((16, KEYS), BF16)
    blocks = [slice(slot * CHIP, (slot + 1) * CHIP) for slot in range(SLOTS)]

    def cols_of(c):
        first = 2 * (c % CHUNKS)
        return [slice((first + i) * DH, (first + i + 1) * DH) for i in range(2)]

    def score_stage(c):
        h, side = c // CHUNKS, c % 2
        query = jnp.concatenate([qb[h, :, col].T for col in cols_of(c)], axis=1)
        raw = jnp.dot(kv[h, :, 0].reshape(KEYS, DH), query, preferred_element_type=F32)
        top = None
        for block in blocks:
            one_bias = bias[block]
            part = raw[block] * (SCALE * math.log2(math.e)) + jnp.concatenate([one_bias, one_bias], axis=1)
            scores[side, block] = part
            part = jnp.max(part.reshape(CHIP // 8, 8, PAIR), axis=0)
            top = part if top is None else jnp.maximum(top, part)
        tops[side] = top

    def out_stage(c):
        h, side = c // CHUNKS, c % 2
        top = jnp.max(tops[side], axis=0, keepdims=True)
        for block in blocks:
            weights[side, block] = jnp.exp2(scores[side, block] - top).astype(BF16)
        out = jnp.dot(value_t[h % 2], weights[side], preferred_element_type=F32)
        inverse = 1.0 / out[DH:DH + 1]
        out = out[:DH] * inverse
        cols = cols_of(c)
        grad = jnp.concatenate([gb[h, :, col].T for col in cols], axis=1)
        grad_t[side] = grad
        delta = jnp.sum(out.astype(BF16).astype(F32) * grad.astype(F32), axis=0, keepdims=True)
        rows[side, 0] = jnp.broadcast_to(inverse, (8, PAIR))
        rows[side, 1] = jnp.broadcast_to(delta, (8, PAIR))
        out = out.T.astype(BF16)
        for i, col in enumerate(cols):
            ob[h, :, col] = out[i * CHIP:(i + 1) * CHIP]

    def change_stage(c):
        h, side = c // CHUNKS, c % 2
        raw = jnp.dot(kv[h, :, 1].reshape(KEYS, DH), grad_t[side], preferred_element_type=F32)
        inverse = jnp.broadcast_to(rows[side, 0, 0:1], (CHIP, PAIR)).astype(BF16)
        delta = rows[side, 1, 0:1]
        for block in blocks:
            prob = weights[side, block] * inverse
            probs[side, block] = prob
            changes[side, block] = prob * (raw[block] - delta).astype(BF16)

    def grad_stage(c):
        h, side = c // CHUNKS, c % 2
        cols = cols_of(c)
        query_grad = (jnp.dot(key_t[h % 2], changes[side], preferred_element_type=F32) * SCALE).T.astype(BF16)
        for i, col in enumerate(cols):
            dqb[h, :, col] = query_grad[i * CHIP:(i + 1) * CHIP]
        for part, (left, right) in enumerate(((changes, qb), (probs, gb))):
            right = jnp.concatenate([right[h, :, col] for col in cols], axis=0)
            total = jnp.dot(left[side], right, preferred_element_type=F32)
            if c % CHUNKS == 0:
                acc[h, part] = total
            else:
                acc[h, part] += total

    def events(h, step):
        if step == 0:
            if h + 1 < HEADS:
                pass_on(h + 1, 2)
            if h + 2 < HEADS:
                own_ahead(h + 2)
                send_rows(h + 2)
        if step == 1 and h >= 2:
            next_sum(h - 2, 4)
        if step == 2 and h >= 1:
            next_sum(h - 1, 1)
        if step == 4:
            if h + 1 < HEADS:
                pass_on(h + 1, 1)
            if h + 2 < HEADS:
                pass_on(h + 2, 3)
            if h >= 1:
                next_sum(h - 1, 2)

    for h in range(HEADS):
        wait_rows(h)
        for slot in (4, 0):
            wait_kv(h, slot, 0)
        key_t[h % 2] = kv[h, :, 0].reshape(KEYS, DH).T
        for step in range(CHUNKS + 3):
            c = h * CHUNKS + step
            if step < CHUNKS:
                score_stage(c)
            if step == 0:
                for slot in (4, 0):
                    wait_kv(h, slot, 1)
                value_t[h % 2, :DH, :] = kv[h, :, 1].reshape(KEYS, DH).T
            if 0 <= step - 2 < CHUNKS:
                change_stage(c - 2)
            if 0 <= step - 1 < CHUNKS:
                out_stage(c - 1)
            if 0 <= step - 3:
                grad_stage(c - 3)
            events(h, step)
        first_sum(h)
        start(out_remote(h))
        keep_out(h)
        if h >= 1:
            next_sum(h - 1, 3)
    for h, slot in ((3, 1), (2, 4), (3, 2), (3, 3), (3, 4)):
        next_sum(h, slot)

    for h in range(HEADS):
        for copy in own_to_ahead(h) + own_to_sibling(h) + rows_to_sibling(h):
            copy.wait_send()
        for part in range(2):
            for slot in (3, 2, 1):
                forward(h, slot, part).wait_send()
            for slot in range(4):
                sum_copy(h, slot, part).wait_send()
        for copy in out_remote(h) + [fin_remote(h, part) for part in range(2)]:
            copy.wait_send()
        for part, dst in enumerate((att_out, dq_out)):
            ref = dst.at[:, head_cols(other, h, WIDE)]
            pltpu.make_async_copy(ref, ref, out_recv.at[h, part]).wait()
        for part, dst in enumerate((dk_out, dv_out)):
            ref = dst.at[:, head_cols(other, h, DH)]
            pltpu.make_async_copy(ref, ref, fin_recv.at[h, part]).wait()


def copy_out(*refs):
    sources, targets, sem = refs[:4], refs[4:8], refs[8]
    copies = []
    for src, dst in zip(sources, targets):
        pieces = 4 if src.shape[1] > 1024 else 1
        step = src.shape[0] // pieces
        for piece in range(pieces):
            rows = pl.ds(piece * step, step)
            copies.append(pltpu.make_async_copy(src.at[rows], dst.at[rows], sem.at[len(copies)]))
    for copy in copies:
        copy.start()
    for copy in copies:
        copy.wait()


def solution(mesh):
    devices = mesh.shape["cp"] * mesh.shape["hd"]
    anywhere = pl.BlockSpec(memory_space=pl.ANY)
    dma = pltpu.SemaphoreType.DMA

    def per_device(queries, key_vectors, value_vectors, out_grad, doc_lengths):
        wide = jax.ShapeDtypeStruct(queries.shape, BF16)
        narrow = jax.ShapeDtypeStruct(key_vectors.shape, BF16)
        results = pl.pallas_call(
            functools.partial(kernel, devices),
            out_shape=tuple(pltpu.VMEM(x.shape, BF16) for x in (wide, wide, narrow, narrow)),
            in_specs=[anywhere] * 5,
            out_specs=(pl.BlockSpec(memory_space=pltpu.VMEM),) * 4,
            scratch_shapes=[
                pltpu.VMEM((HEADS, SLOTS, 2, CHIP, DH), BF16),
                pltpu.VMEM((HEADS, CHIP, WIDE), BF16),
                pltpu.VMEM((HEADS, CHIP, WIDE), BF16),
                pltpu.VMEM((HEADS, CHIP, WIDE), BF16),
                pltpu.VMEM((HEADS, CHIP, WIDE), BF16),
                pltpu.VMEM((HEADS, 2, KEYS, DH), F32),
                pltpu.VMEM((HEADS, 4, 2, CHIP, DH), BF16),
                pltpu.VMEM((HEADS, 4, 2, CHIP, DH), BF16),
                pltpu.VMEM((HEADS, 2, CHIP, DH), BF16),
                pltpu.VMEM((KEYS, DH), F32),
                pltpu.VMEM((1, 128), jnp.int32),
                pltpu.VMEM((2, DH, KEYS), BF16),
                pltpu.VMEM((2, DH + 16, KEYS), BF16),
                pltpu.VMEM((2, DH, PAIR), BF16),
                pltpu.VMEM((2, KEYS, PAIR), F32),
                pltpu.VMEM((2, 8, PAIR), F32),
                pltpu.VMEM((2, 2, 8, PAIR), F32),
                pltpu.VMEM((2, KEYS, PAIR), BF16),
                pltpu.VMEM((2, KEYS, PAIR), BF16),
                pltpu.VMEM((2, KEYS, PAIR), BF16),
                pltpu.VMEM((ROWS, 2 * HEADS * DH), BF16),
                pltpu.VMEM((ROWS, 2 * HEADS * DH), BF16),
                pltpu.VMEM((HEADS, ROWS, WIDE), BF16),
                pltpu.VMEM((HEADS, ROWS, WIDE), BF16),
                dma,
                dma((HEADS, SLOTS, 2)),
                dma((HEADS, 3, 2)),
                dma((HEADS, 2, 2)),
                dma((HEADS, 2)),
                dma((HEADS, 2)),
                dma((HEADS, 2)),
                dma((HEADS, 4, 2)),
                dma((HEADS, 4, 2)),
                dma((HEADS, 2)),
                dma((HEADS, 2)),
                dma((HEADS, 2)),
                dma((HEADS, 2)),
                dma((2,)),
                dma((HEADS, 2)),
            ],
            compiler_params=pltpu.CompilerParams(
                collective_id=0, has_side_effects=True, vmem_limit_bytes=56 * 1024 * 1024
            ),
            cost_estimate=pl.CostEstimate(
                flops=HEADS * GROUP * CHIP * KEYS * DH * 12,
                bytes_accessed=5 * 1024 * 1024,
                transcendentals=HEADS * GROUP * CHIP * KEYS,
            ),
        )(queries, key_vectors, value_vectors, out_grad, doc_lengths.reshape(1, -1))
        return pl.pallas_call(
            copy_out,
            out_shape=(wide, wide, narrow, narrow),
            in_specs=[pl.BlockSpec(memory_space=pltpu.VMEM)] * 4,
            out_specs=(anywhere,) * 4,
            scratch_shapes=[dma((10,))],
            compiler_params=pltpu.CompilerParams(vmem_limit_bytes=8 * 1024 * 1024),
        )(*results)

    token = P(("cp", "hd"), None)
    return jax.shard_map(
        per_device,
        mesh=mesh,
        in_specs=(token, token, token, token, P()),
        out_specs=(token,) * 4,
        check_vma=False,
    )
```

```python
import functools
import math

import jax
import jax.numpy as jnp
from jax import lax
from jax.experimental import pallas as pl
from jax.experimental.pallas import tpu as pltpu
from jax.sharding import PartitionSpec as P

DH = 128
ROWS = 64
CHIP = 2 * ROWS
SLOTS = 5
KEYS = SLOTS * CHIP
HEADS = 4
GROUP = 8
WIDE = GROUP * DH
PAIR = 2 * CHIP
CHUNKS = GROUP // 2
SCALE = DH ** (-0.5)
MESH = pl.DeviceIdType.MESH
F32 = jnp.float32
BF16 = jnp.bfloat16


def kernel(
    devices,
    q_in, k_in, v_in, g_in, len_in,
    att_out, dq_out, dk_out, dv_out,
    kv, qb, gb, ob, dqb, acc, gin, gout, fin, bias, lens,
    key_t, value_t, grad_t, scores, tops, rows, weights, probs, changes,
    k_own, v_own, q_away, g_away,
    len_sem, kv_recv, kv_fwd, own_ici, own_sib,
    qg_recv, qg_send, sum_recv, sum_send,
    out_send, out_recv, fin_send, fin_recv, kv_stage, qg_stage,
):
    cp = lax.axis_index("cp")
    hd = lax.axis_index("hd")
    me = cp * 8 + hd
    core = lax.rem(hd, 2)
    other = 1 - core

    def device(index):
        index = lax.rem(index + devices, devices)
        return (index // 8, lax.rem(index, 8))

    sibling = (cp, hd + 1 - 2 * core)
    chip_base = me - core
    ahead = device(me + 2)
    ahead_other = device(chip_base + 2 + other)
    behind = device(me - 2)
    behind_other = device(chip_base - 2 + other)
    my_rows = pl.ds(pl.multiple_of(core * ROWS, ROWS), ROWS)
    sib_rows = pl.ds(pl.multiple_of(other * ROWS, ROWS), ROWS)

    def head_cols(owner, h, width):
        return pl.ds(pl.multiple_of((owner * HEADS + h) * width, width), width)

    def remote(src, dst, send, recv, target):
        return pltpu.make_async_remote_copy(
            src_ref=src, dst_ref=dst, send_sem=send, recv_sem=recv, device_id=target, device_id_type=MESH
        )

    def own_to_ahead(h):
        made = []
        for side, (owner, target) in enumerate(((core, ahead), (other, ahead_other))):
            for part, src in enumerate((k_own, v_own)):
                made.append(remote(
                    src.at[:, head_cols(owner, h, DH)], kv.at[h, 3, part, my_rows],
                    own_ici.at[h, side, part], kv_recv.at[h, 3, part], target,
                ))
        return made

    def own_to_sibling(h):
        return [
            remote(src.at[:, head_cols(other, h, DH)], kv.at[h, 4, part, my_rows],
                   own_sib.at[h, part], kv_recv.at[h, 4, part], sibling)
            for part, src in enumerate((k_own, v_own))
        ]

    def own_local(h):
        return [
            pltpu.make_async_copy(src.at[:, head_cols(core, h, DH)], kv.at[h, 4, part, my_rows], kv_recv.at[h, 4, part])
            for part, src in enumerate((k_in, v_in))
        ]

    def rows_to_sibling(h):
        return [
            remote(src.at[h], dst.at[h, my_rows], qg_send.at[h, part], qg_recv.at[h, part], sibling)
            for part, (src, dst) in enumerate(((q_away, qb), (g_away, gb)))
        ]

    def stage_kv():
        return [
            pltpu.make_async_copy(src, dst, kv_stage.at[part])
            for part, (src, dst) in enumerate(((k_in, k_own), (v_in, v_own)))
        ]

    def stage_rows(h):
        return [
            pltpu.make_async_copy(src.at[:, head_cols(other, h, WIDE)], dst.at[h], qg_stage.at[h, part])
            for part, (src, dst) in enumerate(((q_in, q_away), (g_in, g_away)))
        ]

    def send_rows(h):
        for copy in stage_rows(h):
            copy.wait()
        start(rows_to_sibling(h))

    def rows_local(h):
        return [
            pltpu.make_async_copy(src.at[:, head_cols(core, h, WIDE)], dst.at[h, my_rows], qg_recv.at[h, part])
            for part, (src, dst) in enumerate(((q_in, qb), (g_in, gb)))
        ]

    def start(copies):
        for copy in copies:
            copy.start()

    def wait_kv(h, slot, part):
        ref = kv.at[h, slot, part]
        pltpu.make_async_copy(ref, ref, kv_recv.at[h, slot, part]).wait()

    def wait_rows(h):
        for part, dst in enumerate((qb, gb)):
            pltpu.make_async_copy(dst.at[h], dst.at[h], qg_recv.at[h, part]).wait()

    def forward(h, slot, part):
        return remote(kv.at[h, slot, part], kv.at[h, slot - 1, part],
                      kv_fwd.at[h, slot - 1, part], kv_recv.at[h, slot - 1, part], ahead)

    def own_ahead(h):
        start(own_to_ahead(h))

    def pass_on(h, slot):
        for part in range(2):
            wait_kv(h, slot, part)
            forward(h, slot, part).start()

    def sum_copy(h, slot, part):
        return remote(gout.at[h, slot, part], gin.at[h, slot, part],
                      sum_send.at[h, slot, part], sum_recv.at[h, slot, part], behind)

    def first_sum(h):
        for part in range(2):
            gout[h, 0, part] = (acc[h, part, 0:CHIP] * (SCALE, 1.0)[part]).astype(BF16)
            sum_copy(h, 0, part).start()

    def next_sum(h, slot):
        for part in range(2):
            ref = gin.at[h, slot - 1, part]
            pltpu.make_async_copy(ref, ref, sum_recv.at[h, slot - 1, part]).wait()
            mine = acc[h, part, slot * CHIP:(slot + 1) * CHIP] * (SCALE, 1.0)[part]
            total = gin[h, slot - 1, part].astype(F32) + mine
            if slot < 4:
                gout[h, slot, part] = total.astype(BF16)
                sum_copy(h, slot, part).start()
            else:
                fin[h, part] = total.astype(BF16)
                fin_remote(h, part).start()
        if slot == 4:
            keep_fin(h)

    def keep_fin(h):
        for part, dst in enumerate((dk_out, dv_out)):
            dst[:, head_cols(core, h, DH)] = fin[h, part, my_rows]

    def fin_remote(h, part):
        return remote(fin.at[h, part, sib_rows], (dk_out, dv_out)[part].at[:, head_cols(core, h, DH)],
                      fin_send.at[h, part], fin_recv.at[h, part], sibling)

    def out_remote(h, part):
        return remote((ob, dqb)[part].at[h, sib_rows], (att_out, dq_out)[part].at[:, head_cols(core, h, WIDE)],
                      out_send.at[h, part], out_recv.at[h, part], sibling)

    def give_out(h, part):
        out_remote(h, part).start()
        (att_out, dq_out)[part][:, head_cols(core, h, WIDE)] = (ob, dqb)[part][h, my_rows]

    barrier = pltpu.get_barrier_semaphore()
    for peer in (sibling, ahead, ahead_other, behind, behind_other):
        pl.semaphore_signal(barrier, inc=1, device_id=peer, device_id_type=MESH)
    len_copy = pltpu.make_async_copy(len_in, lens, len_sem)
    len_copy.start()
    start(stage_kv())
    for h in range(HEADS):
        start(own_local(h))
        start(stage_rows(h))
        start(rows_local(h))
    for copy in stage_kv():
        copy.wait()
    pl.semaphore_wait(barrier, 5)

    for h in range(2):
        own_ahead(h)
    for h in range(HEADS):
        start(own_to_sibling(h))
    send_rows(0)

    len_copy.wait()
    first_pos = (chip_base // 2) * CHIP
    low = lax.broadcasted_iota(jnp.int32, (DH, DH), 0)
    high = lax.broadcasted_iota(jnp.int32, (DH, DH), 1)
    ends_col = jnp.sum(jnp.where(high <= low, lens[...].astype(F32), 0.0), axis=1, keepdims=True)
    ends_row = jnp.sum(jnp.where(low == high, ends_col, 0.0), axis=0, keepdims=True)
    query_pos = high + first_pos
    query_seg = jnp.sum(jnp.where(ends_col <= query_pos.astype(F32), 1.0, 0.0), axis=0, keepdims=True)
    for slot in range(SLOTS):
        key_pos = low + (first_pos - (4 - slot) * CHIP)
        key_seg = jnp.sum(jnp.where(ends_row <= key_pos.astype(F32), 1.0, 0.0), axis=1, keepdims=True)
        allowed = (key_pos >= 0) & (key_pos <= query_pos) & (key_seg == query_seg)
        bias[slot * CHIP:(slot + 1) * CHIP, :] = jnp.where(allowed, 0.0, -1e30)

    pass_on(0, 3)
    send_rows(1)
    pass_on(1, 3)
    pass_on(0, 2)
    own_ahead(2)
    pass_on(1, 2)
    pass_on(0, 1)
    own_ahead(3)
    send_rows(2)
    pass_on(2, 3)
    pass_on(1, 1)
    send_rows(3)

    for side in range(2):
        value_t[side, DH:, :] = jnp.ones((16, KEYS), BF16)
    blocks = [slice(slot * CHIP, (slot + 1) * CHIP) for slot in range(SLOTS)]

    def cols_of(c):
        first = 2 * (c % CHUNKS)
        return [slice((first + i) * DH, (first + i + 1) * DH) for i in range(2)]

    def prepare(h):
        key_t[h] = kv[h, :, 0].reshape(KEYS, DH).T
        value_t[h % 2, :DH, :] = kv[h, :, 1].reshape(KEYS, DH).T

    def score_stage(c):
        h, side = c // CHUNKS, c % 2
        query = jnp.concatenate([qb[h, :, col].T for col in cols_of(c)], axis=1)
        raw = jnp.dot(kv[h, :, 0].reshape(KEYS, DH), query, preferred_element_type=F32)
        top = None
        for block in blocks:
            one_bias = bias[block]
            part = raw[block] * (SCALE * math.log2(math.e)) + jnp.concatenate([one_bias, one_bias], axis=1)
            scores[side, block] = part
            part = jnp.max(part.reshape(CHIP // 8, 8, PAIR), axis=0)
            top = part if top is None else jnp.maximum(top, part)
        tops[side] = top

    def out_stage(c):
        h, side = c // CHUNKS, c % 2
        top = jnp.max(tops[side], axis=0, keepdims=True)
        for block in blocks:
            weights[side, block] = jnp.exp2(scores[side, block] - top).astype(BF16)
        out = jnp.dot(value_t[h % 2], weights[side], preferred_element_type=F32)
        inverse = 1.0 / out[DH:DH + 1]
        out = out[:DH] * inverse
        cols = cols_of(c)
        grad = jnp.concatenate([gb[h, :, col].T for col in cols], axis=1)
        grad_t[side] = grad
        delta = jnp.sum(out.astype(BF16).astype(F32) * grad.astype(F32), axis=0, keepdims=True)
        rows[side, 0] = jnp.broadcast_to(inverse, (8, PAIR))
        rows[side, 1] = jnp.broadcast_to(delta, (8, PAIR))
        out = out.T.astype(BF16)
        for i, col in enumerate(cols):
            ob[h, :, col] = out[i * CHIP:(i + 1) * CHIP]

    def change_stage(c):
        h, side = c // CHUNKS, c % 2
        raw = jnp.dot(kv[h, :, 1].reshape(KEYS, DH), grad_t[side], preferred_element_type=F32)
        inverse = jnp.broadcast_to(rows[side, 0, 0:1], (CHIP, PAIR)).astype(BF16)
        delta = rows[side, 1, 0:1]
        for block in blocks:
            prob = weights[side, block] * inverse
            probs[side, block] = prob
            changes[c, block] = prob * (raw[block] - delta).astype(BF16)

    def key_stage(c):
        h = c // CHUNKS
        for part, (left, right) in enumerate(((changes.at[c], qb), (probs.at[c % 2], gb))):
            right = jnp.concatenate([right[h, :, col] for col in cols_of(c)], axis=0)
            total = jnp.dot(left[...], right, preferred_element_type=F32)
            if c % CHUNKS == 0:
                acc[h, part] = total
            else:
                acc[h, part] += total

    def query_stage(h):
        for c in range(h * CHUNKS, (h + 1) * CHUNKS):
            query_grad = (jnp.dot(key_t[h], changes[c], preferred_element_type=F32) * SCALE).T.astype(BF16)
            for i, col in enumerate(cols_of(c)):
                dqb[h, :, col] = query_grad[i * CHIP:(i + 1) * CHIP]
        give_out(h, 1)

    after = {
        1: [(pass_on, 2, 2), (pass_on, 3, 3)],
        5: [(pass_on, 2, 1), (pass_on, 3, 2)],
        9: [(pass_on, 3, 1)],
        10: [(next_sum, 0, 1)],
        14: [(next_sum, 0, 2), (next_sum, 1, 1)],
    }
    steps = HEADS * CHUNKS
    for step in range(steps + 3):
        if step < steps and step % CHUNKS == 0:
            h = step // CHUNKS
            wait_rows(h)
            for slot in (4, 0):
                for part in range(2):
                    wait_kv(h, slot, part)
            prepare(h)
        if step < steps:
            score_stage(step)
        if 0 <= step - 2 < steps:
            change_stage(step - 2)
        if 0 <= step - 1 < steps:
            out_stage(step - 1)
        if 0 <= step - 3:
            key_stage(step - 3)
            if (step - 3) % CHUNKS == CHUNKS - 1:
                h = (step - 3) // CHUNKS
                first_sum(h)
                give_out(h, 0)
        for event, *where in after.get(step, []):
            event(*where)
    for h, slot in ((0, 3), (1, 2), (2, 1)):
        next_sum(h, slot)
    query_stage(0)
    query_stage(1)
    for h, slot in ((0, 4), (1, 3), (2, 2), (3, 1)):
        next_sum(h, slot)
    query_stage(2)
    query_stage(3)
    for h, slot in ((1, 4), (2, 3), (3, 2), (2, 4), (3, 3), (3, 4)):
        next_sum(h, slot)

    for h in range(HEADS):
        for copy in own_to_ahead(h) + own_to_sibling(h) + rows_to_sibling(h):
            copy.wait_send()
        for part in range(2):
            for slot in (3, 2, 1):
                forward(h, slot, part).wait_send()
            for slot in range(4):
                sum_copy(h, slot, part).wait_send()
            out_remote(h, part).wait_send()
            fin_remote(h, part).wait_send()
        for part, dst in enumerate((att_out, dq_out)):
            ref = dst.at[:, head_cols(other, h, WIDE)]
            pltpu.make_async_copy(ref, ref, out_recv.at[h, part]).wait()
        for part, dst in enumerate((dk_out, dv_out)):
            ref = dst.at[:, head_cols(other, h, DH)]
            pltpu.make_async_copy(ref, ref, fin_recv.at[h, part]).wait()


def copy_out(*refs):
    sources, targets, sem = refs[:4], refs[4:8], refs[8]
    copies = []
    for src, dst in zip(sources, targets):
        pieces = 4 if src.shape[1] > 1024 else 1
        step = src.shape[0] // pieces
        for piece in range(pieces):
            rows = pl.ds(piece * step, step)
            copies.append(pltpu.make_async_copy(src.at[rows], dst.at[rows], sem.at[len(copies)]))
    for copy in copies:
        copy.start()
    for copy in copies:
        copy.wait()


def solution(mesh):
    devices = mesh.shape["cp"] * mesh.shape["hd"]
    anywhere = pl.BlockSpec(memory_space=pl.ANY)
    dma = pltpu.SemaphoreType.DMA

    def per_device(queries, key_vectors, value_vectors, out_grad, doc_lengths):
        wide = jax.ShapeDtypeStruct(queries.shape, BF16)
        narrow = jax.ShapeDtypeStruct(key_vectors.shape, BF16)
        results = pl.pallas_call(
            functools.partial(kernel, devices),
            out_shape=tuple(pltpu.VMEM(x.shape, BF16) for x in (wide, wide, narrow, narrow)),
            in_specs=[anywhere] * 5,
            out_specs=(pl.BlockSpec(memory_space=pltpu.VMEM),) * 4,
            scratch_shapes=[
                pltpu.VMEM((HEADS, SLOTS, 2, CHIP, DH), BF16),
                pltpu.VMEM((HEADS, CHIP, WIDE), BF16),
                pltpu.VMEM((HEADS, CHIP, WIDE), BF16),
                pltpu.VMEM((HEADS, CHIP, WIDE), BF16),
                pltpu.VMEM((HEADS, CHIP, WIDE), BF16),
                pltpu.VMEM((HEADS, 2, KEYS, DH), F32),
                pltpu.VMEM((HEADS, 4, 2, CHIP, DH), BF16),
                pltpu.VMEM((HEADS, 4, 2, CHIP, DH), BF16),
                pltpu.VMEM((HEADS, 2, CHIP, DH), BF16),
                pltpu.VMEM((KEYS, DH), F32),
                pltpu.VMEM((1, 128), jnp.int32),
                pltpu.VMEM((HEADS, DH, KEYS), BF16),
                pltpu.VMEM((2, DH + 16, KEYS), BF16),
                pltpu.VMEM((2, DH, PAIR), BF16),
                pltpu.VMEM((2, KEYS, PAIR), F32),
                pltpu.VMEM((2, 8, PAIR), F32),
                pltpu.VMEM((2, 2, 8, PAIR), F32),
                pltpu.VMEM((2, KEYS, PAIR), BF16),
                pltpu.VMEM((2, KEYS, PAIR), BF16),
                pltpu.VMEM((HEADS * CHUNKS, KEYS, PAIR), BF16),
                pltpu.VMEM((ROWS, 2 * HEADS * DH), BF16),
                pltpu.VMEM((ROWS, 2 * HEADS * DH), BF16),
                pltpu.VMEM((HEADS, ROWS, WIDE), BF16),
                pltpu.VMEM((HEADS, ROWS, WIDE), BF16),
                dma,
                dma((HEADS, SLOTS, 2)),
                dma((HEADS, 3, 2)),
                dma((HEADS, 2, 2)),
                dma((HEADS, 2)),
                dma((HEADS, 2)),
                dma((HEADS, 2)),
                dma((HEADS, 4, 2)),
                dma((HEADS, 4, 2)),
                dma((HEADS, 2)),
                dma((HEADS, 2)),
                dma((HEADS, 2)),
                dma((HEADS, 2)),
                dma((2,)),
                dma((HEADS, 2)),
            ],
            compiler_params=pltpu.CompilerParams(
                collective_id=0, has_side_effects=True, vmem_limit_bytes=56 * 1024 * 1024
            ),
            cost_estimate=pl.CostEstimate(
                flops=HEADS * GROUP * CHIP * KEYS * DH * 12,
                bytes_accessed=5 * 1024 * 1024,
                transcendentals=HEADS * GROUP * CHIP * KEYS,
            ),
        )(queries, key_vectors, value_vectors, out_grad, doc_lengths.reshape(1, -1))
        return pl.pallas_call(
            copy_out,
            out_shape=(wide, wide, narrow, narrow),
            in_specs=[pl.BlockSpec(memory_space=pltpu.VMEM)] * 4,
            out_specs=(anywhere,) * 4,
            scratch_shapes=[dma((10,))],
            compiler_params=pltpu.CompilerParams(vmem_limit_bytes=8 * 1024 * 1024),
        )(*results)

    token = P(("cp", "hd"), None)
    return jax.shard_map(
        per_device,
        mesh=mesh,
        in_specs=(token, token, token, token, P()),
        out_specs=(token,) * 4,
        check_vma=False,
    )
```

```python
import functools
import math

import jax
import jax.numpy as jnp
from jax import lax
from jax.experimental import pallas as pl
from jax.experimental.pallas import tpu as pltpu
from jax.sharding import PartitionSpec as P

DH = 128
ROWS = 64
CHIP = 2 * ROWS
SLOTS = 5
KEYS = SLOTS * CHIP
HEADS = 4
GROUP = 8
WIDE = GROUP * DH
PAIR = 2 * CHIP
CHUNKS = GROUP // 2
SCALE = DH ** (-0.5)
MESH = pl.DeviceIdType.MESH
F32 = jnp.float32
BF16 = jnp.bfloat16


def kernel(
    devices,
    q_in, k_in, v_in, g_in, len_in,
    att_out, dq_out, dk_out, dv_out,
    kv, qb, gb, ob, dqb, acc, gin, gout, fin, bias, lens,
    value_t, grad_t, scores, tops, rows, probs, changes,
    k_own, v_own, q_away, g_away,
    len_sem, kv_recv, kv_fwd, own_ici, own_sib,
    qg_recv, qg_send, sum_recv, sum_send,
    out_send, out_recv, fin_send, fin_recv, kv_stage, qg_stage,
):
    cp = lax.axis_index("cp")
    hd = lax.axis_index("hd")
    me = cp * 8 + hd
    core = lax.rem(hd, 2)
    other = 1 - core

    def device(index):
        index = lax.rem(index + devices, devices)
        return (index // 8, lax.rem(index, 8))

    sibling = (cp, hd + 1 - 2 * core)
    chip_base = me - core
    ahead = device(me + 2)
    ahead_other = device(chip_base + 2 + other)
    behind = device(me - 2)
    behind_other = device(chip_base - 2 + other)
    my_rows = pl.ds(pl.multiple_of(core * ROWS, ROWS), ROWS)
    sib_rows = pl.ds(pl.multiple_of(other * ROWS, ROWS), ROWS)

    def head_cols(owner, h, width):
        return pl.ds(pl.multiple_of((owner * HEADS + h) * width, width), width)

    def remote(src, dst, send, recv, target):
        return pltpu.make_async_remote_copy(
            src_ref=src, dst_ref=dst, send_sem=send, recv_sem=recv, device_id=target, device_id_type=MESH
        )

    def own_to_ahead(h):
        made = []
        for side, (owner, target) in enumerate(((core, ahead), (other, ahead_other))):
            for part, src in enumerate((k_own, v_own)):
                made.append(remote(
                    src.at[:, head_cols(owner, h, DH)], kv.at[h, 3, part, my_rows],
                    own_ici.at[h, side, part], kv_recv.at[h, 3, part], target,
                ))
        return made

    def own_to_sibling(h):
        return [
            remote(src.at[:, head_cols(other, h, DH)], kv.at[h, 4, part, my_rows],
                   own_sib.at[h, part], kv_recv.at[h, 4, part], sibling)
            for part, src in enumerate((k_own, v_own))
        ]

    def own_local(h):
        return [
            pltpu.make_async_copy(src.at[:, head_cols(core, h, DH)], kv.at[h, 4, part, my_rows], kv_recv.at[h, 4, part])
            for part, src in enumerate((k_in, v_in))
        ]

    def rows_to_sibling(h):
        return [
            remote(src.at[h], dst.at[h, my_rows], qg_send.at[h, part], qg_recv.at[h, part], sibling)
            for part, (src, dst) in enumerate(((q_away, qb), (g_away, gb)))
        ]

    def stage_kv():
        return [
            pltpu.make_async_copy(src, dst, kv_stage.at[part])
            for part, (src, dst) in enumerate(((k_in, k_own), (v_in, v_own)))
        ]

    def stage_rows(h):
        return [
            pltpu.make_async_copy(src.at[:, head_cols(other, h, WIDE)], dst.at[h], qg_stage.at[h, part])
            for part, (src, dst) in enumerate(((q_in, q_away), (g_in, g_away)))
        ]

    def send_rows(h):
        for copy in stage_rows(h):
            copy.wait()
        start(rows_to_sibling(h))

    def rows_local(h):
        return [
            pltpu.make_async_copy(src.at[:, head_cols(core, h, WIDE)], dst.at[h, my_rows], qg_recv.at[h, part])
            for part, (src, dst) in enumerate(((q_in, qb), (g_in, gb)))
        ]

    def start(copies):
        for copy in copies:
            copy.start()

    def wait_kv(h, slot, part):
        ref = kv.at[h, slot, part]
        pltpu.make_async_copy(ref, ref, kv_recv.at[h, slot, part]).wait()

    def wait_rows(h):
        for part, dst in enumerate((qb, gb)):
            pltpu.make_async_copy(dst.at[h], dst.at[h], qg_recv.at[h, part]).wait()

    def forward(h, slot, part):
        return remote(kv.at[h, slot, part], kv.at[h, slot - 1, part],
                      kv_fwd.at[h, slot - 1, part], kv_recv.at[h, slot - 1, part], ahead)

    def own_ahead(h):
        start(own_to_ahead(h))

    def pass_on(h, slot, parts=(0, 1)):
        for part in parts:
            wait_kv(h, slot, part)
            forward(h, slot, part).start()

    def sum_copy(h, slot, part):
        return remote(gout.at[h, slot, part], gin.at[h, slot, part],
                      sum_send.at[h, slot, part], sum_recv.at[h, slot, part], behind)

    def first_sum(h, part):
        gout[h, 0, part] = (acc[h, part, 0:CHIP] * (SCALE, 1.0)[part]).astype(BF16)
        sum_copy(h, 0, part).start()

    def next_sum(h, part, slot):
        ref = gin.at[h, slot - 1, part]
        pltpu.make_async_copy(ref, ref, sum_recv.at[h, slot - 1, part]).wait()
        mine = acc[h, part, slot * CHIP:(slot + 1) * CHIP] * (SCALE, 1.0)[part]
        total = gin[h, slot - 1, part].astype(F32) + mine
        if slot < 4:
            gout[h, slot, part] = total.astype(BF16)
            sum_copy(h, slot, part).start()
        else:
            fin[h, part] = total.astype(BF16)
            fin_remote(h, part).start()
            keep_fin(h, part)

    def keep_fin(h, part):
        (dk_out, dv_out)[part][:, head_cols(core, h, DH)] = fin[h, part, my_rows]

    def fin_remote(h, part):
        return remote(fin.at[h, part, sib_rows], (dk_out, dv_out)[part].at[:, head_cols(core, h, DH)],
                      fin_send.at[h, part], fin_recv.at[h, part], sibling)

    def out_remote(h, part):
        return remote((ob, dqb)[part].at[h, sib_rows], (att_out, dq_out)[part].at[:, head_cols(core, h, WIDE)],
                      out_send.at[h, part], out_recv.at[h, part], sibling)

    def give_out(h, part):
        out_remote(h, part).start()
        (att_out, dq_out)[part][:, head_cols(core, h, WIDE)] = (ob, dqb)[part][h, my_rows]

    barrier = pltpu.get_barrier_semaphore()
    for peer in (sibling, ahead, ahead_other, behind, behind_other):
        pl.semaphore_signal(barrier, inc=1, device_id=peer, device_id_type=MESH)
    len_copy = pltpu.make_async_copy(len_in, lens, len_sem)
    len_copy.start()
    start(stage_kv())
    for h in range(HEADS):
        start(own_local(h))
        start(stage_rows(h))
        start(rows_local(h))
    for copy in stage_kv():
        copy.wait()
    pl.semaphore_wait(barrier, 5)

    for h in range(2):
        own_ahead(h)
    for h in range(HEADS):
        start(own_to_sibling(h))
    send_rows(0)

    len_copy.wait()
    first_pos = (chip_base // 2) * CHIP
    low = lax.broadcasted_iota(jnp.int32, (DH, DH), 0)
    high = lax.broadcasted_iota(jnp.int32, (DH, DH), 1)
    ends_col = jnp.sum(jnp.where(high <= low, lens[...].astype(F32), 0.0), axis=1, keepdims=True)
    ends_row = jnp.sum(jnp.where(low == high, ends_col, 0.0), axis=0, keepdims=True)
    query_pos = high + first_pos
    query_seg = jnp.sum(jnp.where(ends_col <= query_pos.astype(F32), 1.0, 0.0), axis=0, keepdims=True)
    for slot in range(SLOTS):
        key_pos = low + (first_pos - (4 - slot) * CHIP)
        key_seg = jnp.sum(jnp.where(ends_row <= key_pos.astype(F32), 1.0, 0.0), axis=1, keepdims=True)
        allowed = (key_pos >= 0) & (key_pos <= query_pos) & (key_seg == query_seg)
        bias[slot * CHIP:(slot + 1) * CHIP, :] = jnp.where(allowed, 0.0, -1e30)

    pass_on(0, 3)
    send_rows(1)
    pass_on(1, 3)
    pass_on(0, 2)
    own_ahead(2)
    pass_on(1, 2)
    pass_on(0, 1)
    own_ahead(3)
    send_rows(2)
    pass_on(2, 3)
    pass_on(1, 1)
    send_rows(3)

    blocks = [slice(slot * CHIP, (slot + 1) * CHIP) for slot in range(SLOTS)]

    def cols_of(c):
        first = 2 * (c % CHUNKS)
        return [slice((first + i) * DH, (first + i + 1) * DH) for i in range(2)]

    def score_stage(c):
        h, side = c // CHUNKS, c % 2
        query = jnp.concatenate([qb[h, :, col].T for col in cols_of(c)], axis=1)
        raw = jnp.dot(kv[h, :, 0].reshape(KEYS, DH), query, preferred_element_type=F32)
        top = None
        for block in blocks:
            one_bias = bias[block]
            part = raw[block] * (SCALE * math.log2(math.e)) + jnp.concatenate([one_bias, one_bias], axis=1)
            scores[side, block] = part
            part = jnp.max(part.reshape(CHIP // 8, 8, PAIR), axis=0)
            top = part if top is None else jnp.maximum(top, part)
        tops[side] = top

    def weight_stage(c):
        side = c % 2
        top = jnp.max(tops[side], axis=0, keepdims=True)
        total = None
        for block in blocks:
            part = jnp.exp2(scores[side, block] - top)
            probs[c, block] = part.astype(BF16)
            part = jnp.sum(part.reshape(CHIP // 8, 8, PAIR), axis=0)
            total = part if total is None else total + part
        inverse = 1.0 / jnp.sum(total, axis=0, keepdims=True)
        inverse = jnp.broadcast_to(inverse, (CHIP, PAIR)).astype(BF16)
        for block in blocks:
            probs[c, block] = probs[c, block] * inverse

    def sum_stage(c, part):
        h = c // CHUNKS
        left, right = ((changes, qb), (probs, gb))[part]
        right = jnp.concatenate([right[h, :, col] for col in cols_of(c)], axis=0)
        total = jnp.dot(left[c], right, preferred_element_type=F32)
        if c % CHUNKS == 0:
            acc[h, part] = total
        else:
            acc[h, part] += total

    def out_stage(c):
        h, side = c // CHUNKS, c % 2
        out = jnp.dot(value_t[h % 2], probs[c], preferred_element_type=F32)
        cols = cols_of(c)
        grad = jnp.concatenate([gb[h, :, col].T for col in cols], axis=1)
        grad_t[side] = grad
        delta = jnp.sum(out.astype(BF16).astype(F32) * grad.astype(F32), axis=0, keepdims=True)
        rows[side] = jnp.broadcast_to(delta, (8, PAIR))
        out = out.T.astype(BF16)
        for i, col in enumerate(cols):
            ob[h, :, col] = out[i * CHIP:(i + 1) * CHIP]

    def change_stage(c):
        h, side = c // CHUNKS, c % 2
        raw = jnp.dot(kv[h, :, 1].reshape(KEYS, DH), grad_t[side], preferred_element_type=F32)
        delta = rows[side, 0:1]
        for block in blocks:
            changes[c, block] = probs[c, block] * (raw[block] - delta).astype(BF16)

    def query_stage(h):
        keys_t = kv[h, :, 0].reshape(KEYS, DH).T
        for c in range(h * CHUNKS, (h + 1) * CHUNKS):
            query_grad = (jnp.dot(keys_t, changes[c], preferred_element_type=F32) * SCALE).T.astype(BF16)
            for i, col in enumerate(cols_of(c)):
                dqb[h, :, col] = query_grad[i * CHIP:(i + 1) * CHIP]
        give_out(h, 1)

    def begin(h, part):
        if part == 0:
            wait_rows(h)
        for slot in (4, 0):
            wait_kv(h, slot, part)
        if part == 1:
            value_t[h % 2] = kv[h, :, 1].reshape(KEYS, DH).T

    def finish(h, part):
        first_sum(h, 1 - part)
        if part == 1:
            give_out(h, 0)

    def run(phases, after):
        items = [(h, part, h * CHUNKS + p) for h, part in phases for p in range(CHUNKS)]
        for step in range(len(items) + 2):
            if step < len(items):
                h, part, c = items[step]
                if c % CHUNKS == 0:
                    begin(h, part)
                (score_stage, out_stage)[part](c)
            if 0 <= step - 1 < len(items):
                h, part, c = items[step - 1]
                (weight_stage, change_stage)[part](c)
            if 0 <= step - 2:
                h, part, c = items[step - 2]
                sum_stage(c, 1 - part)
                if c % CHUNKS == CHUNKS - 1:
                    finish(h, part)
            for event, *where in after.get(step, []):
                event(*where)

    key, value = 0, 1
    run(((0, 0), (0, 1), (1, 0), (1, 1)), {
        3: [(pass_on, 2, 2, (key,)), (pass_on, 3, 3, (key,)), (pass_on, 2, 2, (value,)), (pass_on, 3, 3, (value,))],
        11: [(pass_on, 2, 1, (key,)), (pass_on, 3, 2, (key,)), (pass_on, 2, 1, (value,)), (pass_on, 3, 2, (value,))],
        14: [(next_sum, 0, value, 1)],
        17: [(next_sum, 0, key, 1)],
    })
    pass_on(3, 1)
    next_sum(1, value, 1)
    next_sum(0, value, 2)
    next_sum(1, key, 1)
    run(((2, 0), (3, 0), (2, 1), (3, 1)), {
        0: [(next_sum, 0, key, 2)],
        4: [(next_sum, 1, value, 2)],
        5: [(next_sum, 0, value, 3)],
        8: [(next_sum, 1, key, 2)],
        9: [(next_sum, 0, key, 3)],
        13: [(next_sum, 1, value, 3)],
        14: [(next_sum, 0, value, 4)],
        15: [(next_sum, 2, value, 1)],
        17: [(next_sum, 1, key, 3)],
    })
    for event, *where in (
        (next_sum, 0, key, 4), (next_sum, 3, value, 1), (query_stage, 0), (next_sum, 1, value, 4),
        (next_sum, 2, key, 1), (next_sum, 2, value, 2), (query_stage, 1), (next_sum, 1, key, 4),
        (next_sum, 3, key, 1), (next_sum, 3, value, 2), (query_stage, 2), (next_sum, 2, key, 2),
        (next_sum, 2, value, 3), (query_stage, 3), (next_sum, 3, key, 2), (next_sum, 3, value, 3),
        (next_sum, 2, key, 3), (next_sum, 2, value, 4), (next_sum, 3, key, 3), (next_sum, 3, value, 4),
        (next_sum, 2, key, 4), (next_sum, 3, key, 4),
    ):
        event(*where)

    for h in range(HEADS):
        for copy in own_to_ahead(h) + own_to_sibling(h) + rows_to_sibling(h):
            copy.wait_send()
        for part in range(2):
            for slot in (3, 2, 1):
                forward(h, slot, part).wait_send()
            for slot in range(4):
                sum_copy(h, slot, part).wait_send()
            out_remote(h, part).wait_send()
            fin_remote(h, part).wait_send()
        for part, dst in enumerate((att_out, dq_out)):
            ref = dst.at[:, head_cols(other, h, WIDE)]
            pltpu.make_async_copy(ref, ref, out_recv.at[h, part]).wait()
        for part, dst in enumerate((dk_out, dv_out)):
            ref = dst.at[:, head_cols(other, h, DH)]
            pltpu.make_async_copy(ref, ref, fin_recv.at[h, part]).wait()


def copy_out(*refs):
    sources, targets, sem = refs[:4], refs[4:8], refs[8]
    copies = []
    for src, dst in zip(sources, targets):
        pieces = 4 if src.shape[1] > 1024 else 1
        step = src.shape[0] // pieces
        for piece in range(pieces):
            rows = pl.ds(piece * step, step)
            copies.append(pltpu.make_async_copy(src.at[rows], dst.at[rows], sem.at[len(copies)]))
    for copy in copies:
        copy.start()
    for copy in copies:
        copy.wait()


def solution(mesh):
    devices = mesh.shape["cp"] * mesh.shape["hd"]
    anywhere = pl.BlockSpec(memory_space=pl.ANY)
    dma = pltpu.SemaphoreType.DMA

    def per_device(queries, key_vectors, value_vectors, out_grad, doc_lengths):
        wide = jax.ShapeDtypeStruct(queries.shape, BF16)
        narrow = jax.ShapeDtypeStruct(key_vectors.shape, BF16)
        results = pl.pallas_call(
            functools.partial(kernel, devices),
            out_shape=tuple(pltpu.VMEM(x.shape, BF16) for x in (wide, wide, narrow, narrow)),
            in_specs=[anywhere] * 5,
            out_specs=(pl.BlockSpec(memory_space=pltpu.VMEM),) * 4,
            scratch_shapes=[
                pltpu.VMEM((HEADS, SLOTS, 2, CHIP, DH), BF16),
                pltpu.VMEM((HEADS, CHIP, WIDE), BF16),
                pltpu.VMEM((HEADS, CHIP, WIDE), BF16),
                pltpu.VMEM((HEADS, CHIP, WIDE), BF16),
                pltpu.VMEM((HEADS, CHIP, WIDE), BF16),
                pltpu.VMEM((HEADS, 2, KEYS, DH), F32),
                pltpu.VMEM((HEADS, 4, 2, CHIP, DH), BF16),
                pltpu.VMEM((HEADS, 4, 2, CHIP, DH), BF16),
                pltpu.VMEM((HEADS, 2, CHIP, DH), BF16),
                pltpu.VMEM((KEYS, DH), F32),
                pltpu.VMEM((1, 128), jnp.int32),
                pltpu.VMEM((2, DH, KEYS), BF16),
                pltpu.VMEM((2, DH, PAIR), BF16),
                pltpu.VMEM((2, KEYS, PAIR), F32),
                pltpu.VMEM((2, 8, PAIR), F32),
                pltpu.VMEM((2, 8, PAIR), F32),
                pltpu.VMEM((HEADS * CHUNKS, KEYS, PAIR), BF16),
                pltpu.VMEM((HEADS * CHUNKS, KEYS, PAIR), BF16),
                pltpu.VMEM((ROWS, 2 * HEADS * DH), BF16),
                pltpu.VMEM((ROWS, 2 * HEADS * DH), BF16),
                pltpu.VMEM((HEADS, ROWS, WIDE), BF16),
                pltpu.VMEM((HEADS, ROWS, WIDE), BF16),
                dma,
                dma((HEADS, SLOTS, 2)),
                dma((HEADS, 3, 2)),
                dma((HEADS, 2, 2)),
                dma((HEADS, 2)),
                dma((HEADS, 2)),
                dma((HEADS, 2)),
                dma((HEADS, 4, 2)),
                dma((HEADS, 4, 2)),
                dma((HEADS, 2)),
                dma((HEADS, 2)),
                dma((HEADS, 2)),
                dma((HEADS, 2)),
                dma((2,)),
                dma((HEADS, 2)),
            ],
            compiler_params=pltpu.CompilerParams(
                collective_id=0, has_side_effects=True, vmem_limit_bytes=56 * 1024 * 1024
            ),
            cost_estimate=pl.CostEstimate(
                flops=HEADS * GROUP * CHIP * KEYS * DH * 12,
                bytes_accessed=5 * 1024 * 1024,
                transcendentals=HEADS * GROUP * CHIP * KEYS,
            ),
        )(queries, key_vectors, value_vectors, out_grad, doc_lengths.reshape(1, -1))
        return pl.pallas_call(
            copy_out,
            out_shape=(wide, wide, narrow, narrow),
            in_specs=[pl.BlockSpec(memory_space=pltpu.VMEM)] * 4,
            out_specs=(anywhere,) * 4,
            scratch_shapes=[dma((10,))],
            compiler_params=pltpu.CompilerParams(vmem_limit_bytes=8 * 1024 * 1024),
        )(*results)

    token = P(("cp", "hd"), None)
    return jax.shard_map(
        per_device,
        mesh=mesh,
        in_specs=(token, token, token, token, P()),
        out_specs=(token,) * 4,
        check_vma=False,
    )
```

```python
import functools
import math

import jax
import jax.numpy as jnp
from jax import lax
from jax.experimental import pallas as pl
from jax.experimental.pallas import tpu as pltpu
from jax.sharding import PartitionSpec as P

DH = 128
ROWS = 64
CHIP = 2 * ROWS
SLOTS = 5
KEYS = SLOTS * CHIP
HEADS = 4
GROUP = 8
WIDE = GROUP * DH
PAIR = 2 * CHIP
CHUNKS = GROUP // 2
SCALE = DH ** (-0.5)
MESH = pl.DeviceIdType.MESH
F32 = jnp.float32
BF16 = jnp.bfloat16


def kernel(
    devices,
    q_in, k_in, v_in, g_in, len_in,
    att_out, dq_out, dk_out, dv_out,
    kv, qb, gb, ob, dqb, acc, gin, gout, fin, bias, lens,
    value_t, grad_t, scores, tops, rows, probs, changes,
    k_own, v_own, q_away, g_away,
    len_sem, kv_recv, kv_fwd, own_ici, own_sib,
    qg_recv, qg_send, sum_recv, sum_send,
    out_send, out_recv, fin_send, fin_recv, kv_stage, qg_stage,
):
    cp = lax.axis_index("cp")
    hd = lax.axis_index("hd")
    me = cp * 8 + hd
    core = lax.rem(hd, 2)
    other = 1 - core

    def device(index):
        index = lax.rem(index + devices, devices)
        return (index // 8, lax.rem(index, 8))

    sibling = (cp, hd + 1 - 2 * core)
    chip_base = me - core
    ahead = device(me + 2)
    ahead_other = device(chip_base + 2 + other)
    behind = device(me - 2)
    behind_other = device(chip_base - 2 + other)
    my_rows = pl.ds(pl.multiple_of(core * ROWS, ROWS), ROWS)
    sib_rows = pl.ds(pl.multiple_of(other * ROWS, ROWS), ROWS)

    def head_cols(owner, h, width):
        return pl.ds(pl.multiple_of((owner * HEADS + h) * width, width), width)

    def remote(src, dst, send, recv, target):
        return pltpu.make_async_remote_copy(
            src_ref=src, dst_ref=dst, send_sem=send, recv_sem=recv, device_id=target, device_id_type=MESH
        )

    def own_to_ahead(h):
        made = []
        for part, src in enumerate((k_own, v_own)):
            for side, (owner, target) in enumerate(((core, ahead), (other, ahead_other))):
                made.append(remote(
                    src.at[:, head_cols(owner, h, DH)], kv.at[h, 3, part, my_rows],
                    own_ici.at[h, side, part], kv_recv.at[h, 3, part], target,
                ))
        return made

    def own_to_sibling(h):
        return [
            remote(src.at[:, head_cols(other, h, DH)], kv.at[h, 4, part, my_rows],
                   own_sib.at[h, part], kv_recv.at[h, 4, part], sibling)
            for part, src in enumerate((k_own, v_own))
        ]

    def own_local(h):
        return [
            pltpu.make_async_copy(src.at[:, head_cols(core, h, DH)], kv.at[h, 4, part, my_rows], kv_recv.at[h, 4, part])
            for part, src in enumerate((k_in, v_in))
        ]

    def rows_to_sibling(h):
        return [
            remote(src.at[h], dst.at[h, my_rows], qg_send.at[h, part], qg_recv.at[h, part], sibling)
            for part, (src, dst) in enumerate(((q_away, qb), (g_away, gb)))
        ]

    def stage_kv():
        return [
            pltpu.make_async_copy(src, dst, kv_stage.at[part])
            for part, (src, dst) in enumerate(((k_in, k_own), (v_in, v_own)))
        ]

    def stage_rows(h):
        return [
            pltpu.make_async_copy(src.at[:, head_cols(other, h, WIDE)], dst.at[h], qg_stage.at[h, part])
            for part, (src, dst) in enumerate(((q_in, q_away), (g_in, g_away)))
        ]

    def send_rows(h):
        for copy in stage_rows(h):
            copy.wait()
        start(rows_to_sibling(h))

    def rows_local(h):
        return [
            pltpu.make_async_copy(src.at[:, head_cols(core, h, WIDE)], dst.at[h, my_rows], qg_recv.at[h, part])
            for part, (src, dst) in enumerate(((q_in, qb), (g_in, gb)))
        ]

    def start(copies):
        for copy in copies:
            copy.start()

    def wait_kv(h, slot, part):
        ref = kv.at[h, slot, part]
        pltpu.make_async_copy(ref, ref, kv_recv.at[h, slot, part]).wait()

    def wait_rows(h):
        for part, dst in enumerate((qb, gb)):
            pltpu.make_async_copy(dst.at[h], dst.at[h], qg_recv.at[h, part]).wait()

    def forward(h, slot, part):
        return remote(kv.at[h, slot, part], kv.at[h, slot - 1, part],
                      kv_fwd.at[h, slot - 1, part], kv_recv.at[h, slot - 1, part], ahead)

    def own_ahead(h):
        start(own_to_ahead(h))

    def pass_on(h, slot, parts=(0, 1)):
        for part in parts:
            wait_kv(h, slot, part)
            forward(h, slot, part).start()

    def sum_copy(h, slot, part):
        return remote(gout.at[h, slot, part], gin.at[h, slot, part],
                      sum_send.at[h, slot, part], sum_recv.at[h, slot, part], behind)

    def first_sum(h, part):
        gout[h, 0, part] = (acc[h, part, 0:CHIP] * (SCALE, 1.0)[part]).astype(BF16)
        sum_copy(h, 0, part).start()

    def next_sum(h, part, slot):
        ref = gin.at[h, slot - 1, part]
        pltpu.make_async_copy(ref, ref, sum_recv.at[h, slot - 1, part]).wait()
        mine = acc[h, part, slot * CHIP:(slot + 1) * CHIP] * (SCALE, 1.0)[part]
        total = gin[h, slot - 1, part].astype(F32) + mine
        if slot < 4:
            gout[h, slot, part] = total.astype(BF16)
            sum_copy(h, slot, part).start()
        else:
            fin[h, part] = total.astype(BF16)
            fin_remote(h, part).start()
            keep_fin(h, part)

    def keep_fin(h, part):
        (dk_out, dv_out)[part][:, head_cols(core, h, DH)] = fin[h, part, my_rows]

    def fin_remote(h, part):
        return remote(fin.at[h, part, sib_rows], (dk_out, dv_out)[part].at[:, head_cols(core, h, DH)],
                      fin_send.at[h, part], fin_recv.at[h, part], sibling)

    def out_remote(h, part):
        return remote((ob, dqb)[part].at[h, sib_rows], (att_out, dq_out)[part].at[:, head_cols(core, h, WIDE)],
                      out_send.at[h, part], out_recv.at[h, part], sibling)

    def give_out(h, part):
        out_remote(h, part).start()
        (att_out, dq_out)[part][:, head_cols(core, h, WIDE)] = (ob, dqb)[part][h, my_rows]

    barrier = pltpu.get_barrier_semaphore()
    for peer in (sibling, ahead, ahead_other, behind, behind_other):
        pl.semaphore_signal(barrier, inc=1, device_id=peer, device_id_type=MESH)
    len_copy = pltpu.make_async_copy(len_in, lens, len_sem)
    len_copy.start()
    start(stage_kv())
    for h in range(HEADS):
        start(own_local(h))
        start(stage_rows(h))
        start(rows_local(h))
    for copy in stage_kv():
        copy.wait()
    pl.semaphore_wait(barrier, 5)

    for h in range(2):
        own_ahead(h)
    for h in range(HEADS):
        start(own_to_sibling(h))
    send_rows(0)

    len_copy.wait()
    first_pos = (chip_base // 2) * CHIP
    low = lax.broadcasted_iota(jnp.int32, (DH, DH), 0)
    high = lax.broadcasted_iota(jnp.int32, (DH, DH), 1)
    ends_col = jnp.sum(jnp.where(high <= low, lens[...].astype(F32), 0.0), axis=1, keepdims=True)
    ends_row = jnp.sum(jnp.where(low == high, ends_col, 0.0), axis=0, keepdims=True)
    query_pos = high + first_pos
    query_seg = jnp.sum(jnp.where(ends_col <= query_pos.astype(F32), 1.0, 0.0), axis=0, keepdims=True)
    for slot in range(SLOTS):
        key_pos = low + (first_pos - (4 - slot) * CHIP)
        key_seg = jnp.sum(jnp.where(ends_row <= key_pos.astype(F32), 1.0, 0.0), axis=1, keepdims=True)
        allowed = (key_pos >= 0) & (key_pos <= query_pos) & (key_seg == query_seg)
        bias[slot * CHIP:(slot + 1) * CHIP, :] = jnp.where(allowed, 0.0, -1e30)

    pass_on(0, 3)
    send_rows(1)
    pass_on(1, 3)
    pass_on(0, 2)
    own_ahead(2)
    pass_on(1, 2)
    pass_on(0, 1)
    own_ahead(3)
    send_rows(2)
    pass_on(2, 3)
    pass_on(1, 1)
    send_rows(3)

    blocks = [slice(slot * CHIP, (slot + 1) * CHIP) for slot in range(SLOTS)]

    def cols_of(c):
        first = 2 * (c % CHUNKS)
        return [slice((first + i) * DH, (first + i + 1) * DH) for i in range(2)]

    def score_stage(c):
        h, side = c // CHUNKS, c % 2
        query = jnp.concatenate([qb[h, :, col].T for col in cols_of(c)], axis=1)
        raw = jnp.dot(kv[h, :, 0].reshape(KEYS, DH), query, preferred_element_type=F32)
        top = None
        for block in blocks:
            one_bias = bias[block]
            part = raw[block] * (SCALE * math.log2(math.e)) + jnp.concatenate([one_bias, one_bias], axis=1)
            scores[side, block] = part
            part = jnp.max(part.reshape(CHIP // 8, 8, PAIR), axis=0)
            top = part if top is None else jnp.maximum(top, part)
        tops[side] = top

    def weight_stage(c):
        side = c % 2
        top = jnp.max(tops[side], axis=0, keepdims=True)
        total = None
        for block in blocks:
            part = jnp.exp2(scores[side, block] - top)
            probs[c, block] = part.astype(BF16)
            part = jnp.sum(part.reshape(CHIP // 8, 8, PAIR), axis=0)
            total = part if total is None else total + part
        inverse = 1.0 / jnp.sum(total, axis=0, keepdims=True)
        inverse = jnp.broadcast_to(inverse, (CHIP, PAIR)).astype(BF16)
        for block in blocks:
            probs[c, block] = probs[c, block] * inverse

    def sum_stage(c, part):
        h = c // CHUNKS
        left, right = ((changes, qb), (probs, gb))[part]
        right = jnp.concatenate([right[h, :, col] for col in cols_of(c)], axis=0)
        total = jnp.dot(left[c], right, preferred_element_type=F32)
        if c % CHUNKS == 0:
            acc[h, part] = total
        else:
            acc[h, part] += total

    def out_stage(c):
        h, side = c // CHUNKS, c % 2
        out = jnp.dot(value_t[h % 2], probs[c], preferred_element_type=F32)
        cols = cols_of(c)
        grad = jnp.concatenate([gb[h, :, col].T for col in cols], axis=1)
        grad_t[side] = grad
        delta = jnp.sum(out.astype(BF16).astype(F32) * grad.astype(F32), axis=0, keepdims=True)
        rows[side] = jnp.broadcast_to(delta, (8, PAIR))
        out = out.T.astype(BF16)
        for i, col in enumerate(cols):
            ob[h, :, col] = out[i * CHIP:(i + 1) * CHIP]

    def change_stage(c):
        h, side = c // CHUNKS, c % 2
        raw = jnp.dot(kv[h, :, 1].reshape(KEYS, DH), grad_t[side], preferred_element_type=F32)
        delta = rows[side, 0:1]
        for block in blocks:
            changes[c, block] = probs[c, block] * (raw[block] - delta).astype(BF16)

    def query_stage(h):
        keys_t = kv[h, :, 0].reshape(KEYS, DH).T
        for c in range(h * CHUNKS, (h + 1) * CHUNKS):
            query_grad = (jnp.dot(keys_t, changes[c], preferred_element_type=F32) * SCALE).T.astype(BF16)
            for i, col in enumerate(cols_of(c)):
                dqb[h, :, col] = query_grad[i * CHIP:(i + 1) * CHIP]
        give_out(h, 1)

    def begin(h, part):
        if part == 0:
            wait_rows(h)
        for slot in (4, 0):
            wait_kv(h, slot, part)
        if part == 1:
            value_t[h % 2] = kv[h, :, 1].reshape(KEYS, DH).T

    def finish(h, part):
        first_sum(h, 1 - part)
        if part == 1:
            give_out(h, 0)

    def run(phases, after):
        items = [(h, part, h * CHUNKS + p) for h, part in phases for p in range(CHUNKS)]
        for step in range(len(items) + 2):
            if step < len(items):
                h, part, c = items[step]
                if c % CHUNKS == 0:
                    begin(h, part)
                (score_stage, out_stage)[part](c)
            if 0 <= step - 1 < len(items):
                h, part, c = items[step - 1]
                (weight_stage, change_stage)[part](c)
            if 0 <= step - 2:
                h, part, c = items[step - 2]
                sum_stage(c, 1 - part)
                if c % CHUNKS == CHUNKS - 1:
                    finish(h, part)
            for event, *where in after.get(step, []):
                event(*where)

    key, value = 0, 1
    run(((0, 0), (0, 1), (1, 0), (1, 1)), {
        5: [(pass_on, 2, 2, (key,)), (pass_on, 3, 3, (key,)), (pass_on, 2, 2, (value,)), (pass_on, 3, 3, (value,))],
        13: [(pass_on, 2, 1, (key,)), (pass_on, 3, 2, (key,)), (pass_on, 2, 1, (value,)), (pass_on, 3, 2, (value,))],
        14: [(next_sum, 0, value, 1)],
        17: [(next_sum, 0, key, 1)],
    })
    pass_on(3, 1)
    next_sum(1, value, 1)
    next_sum(0, value, 2)
    next_sum(1, key, 1)
    run(((2, 0), (3, 0), (2, 1), (3, 1)), {
        2: [(next_sum, 0, key, 2)],
        6: [(next_sum, 1, value, 2)],
        7: [(next_sum, 0, value, 3)],
        10: [(next_sum, 1, key, 2)],
        11: [(next_sum, 0, key, 3)],
        15: [(next_sum, 1, value, 3)],
        16: [(next_sum, 0, value, 4)],
        17: [(next_sum, 2, value, 1), (next_sum, 1, key, 3)],
    })
    for event, *where in (
        (next_sum, 0, key, 4), (next_sum, 3, value, 1), (query_stage, 0), (next_sum, 1, value, 4),
        (next_sum, 2, key, 1), (next_sum, 2, value, 2), (query_stage, 1), (next_sum, 1, key, 4),
        (next_sum, 3, key, 1), (next_sum, 3, value, 2), (query_stage, 2), (next_sum, 2, key, 2),
        (next_sum, 2, value, 3), (query_stage, 3), (next_sum, 3, key, 2), (next_sum, 3, value, 3),
        (next_sum, 2, key, 3), (next_sum, 2, value, 4), (next_sum, 3, key, 3), (next_sum, 3, value, 4),
        (next_sum, 2, key, 4), (next_sum, 3, key, 4),
    ):
        event(*where)

    for h in range(HEADS):
        for copy in own_to_ahead(h) + own_to_sibling(h) + rows_to_sibling(h):
            copy.wait_send()
        for part in range(2):
            for slot in (3, 2, 1):
                forward(h, slot, part).wait_send()
            for slot in range(4):
                sum_copy(h, slot, part).wait_send()
            out_remote(h, part).wait_send()
            fin_remote(h, part).wait_send()
        for part, dst in enumerate((att_out, dq_out)):
            ref = dst.at[:, head_cols(other, h, WIDE)]
            pltpu.make_async_copy(ref, ref, out_recv.at[h, part]).wait()
        for part, dst in enumerate((dk_out, dv_out)):
            ref = dst.at[:, head_cols(other, h, DH)]
            pltpu.make_async_copy(ref, ref, fin_recv.at[h, part]).wait()


def copy_out(*refs):
    sources, targets, sem = refs[:4], refs[4:8], refs[8]
    copies = []
    for src, dst in zip(sources, targets):
        pieces = 4 if src.shape[1] > 1024 else 1
        step = src.shape[0] // pieces
        for piece in range(pieces):
            rows = pl.ds(piece * step, step)
            copies.append(pltpu.make_async_copy(src.at[rows], dst.at[rows], sem.at[len(copies)]))
    for copy in copies:
        copy.start()
    for copy in copies:
        copy.wait()


def solution(mesh):
    devices = mesh.shape["cp"] * mesh.shape["hd"]
    anywhere = pl.BlockSpec(memory_space=pl.ANY)
    dma = pltpu.SemaphoreType.DMA

    def per_device(queries, key_vectors, value_vectors, out_grad, doc_lengths):
        wide = jax.ShapeDtypeStruct(queries.shape, BF16)
        narrow = jax.ShapeDtypeStruct(key_vectors.shape, BF16)
        results = pl.pallas_call(
            functools.partial(kernel, devices),
            out_shape=tuple(pltpu.VMEM(x.shape, BF16) for x in (wide, wide, narrow, narrow)),
            in_specs=[anywhere] * 5,
            out_specs=(pl.BlockSpec(memory_space=pltpu.VMEM),) * 4,
            scratch_shapes=[
                pltpu.VMEM((HEADS, SLOTS, 2, CHIP, DH), BF16),
                pltpu.VMEM((HEADS, CHIP, WIDE), BF16),
                pltpu.VMEM((HEADS, CHIP, WIDE), BF16),
                pltpu.VMEM((HEADS, CHIP, WIDE), BF16),
                pltpu.VMEM((HEADS, CHIP, WIDE), BF16),
                pltpu.VMEM((HEADS, 2, KEYS, DH), F32),
                pltpu.VMEM((HEADS, 4, 2, CHIP, DH), BF16),
                pltpu.VMEM((HEADS, 4, 2, CHIP, DH), BF16),
                pltpu.VMEM((HEADS, 2, CHIP, DH), BF16),
                pltpu.VMEM((KEYS, DH), F32),
                pltpu.VMEM((1, 128), jnp.int32),
                pltpu.VMEM((2, DH, KEYS), BF16),
                pltpu.VMEM((2, DH, PAIR), BF16),
                pltpu.VMEM((2, KEYS, PAIR), F32),
                pltpu.VMEM((2, 8, PAIR), F32),
                pltpu.VMEM((2, 8, PAIR), F32),
                pltpu.VMEM((HEADS * CHUNKS, KEYS, PAIR), BF16),
                pltpu.VMEM((HEADS * CHUNKS, KEYS, PAIR), BF16),
                pltpu.VMEM((ROWS, 2 * HEADS * DH), BF16),
                pltpu.VMEM((ROWS, 2 * HEADS * DH), BF16),
                pltpu.VMEM((HEADS, ROWS, WIDE), BF16),
                pltpu.VMEM((HEADS, ROWS, WIDE), BF16),
                dma,
                dma((HEADS, SLOTS, 2)),
                dma((HEADS, 3, 2)),
                dma((HEADS, 2, 2)),
                dma((HEADS, 2)),
                dma((HEADS, 2)),
                dma((HEADS, 2)),
                dma((HEADS, 4, 2)),
                dma((HEADS, 4, 2)),
                dma((HEADS, 2)),
                dma((HEADS, 2)),
                dma((HEADS, 2)),
                dma((HEADS, 2)),
                dma((2,)),
                dma((HEADS, 2)),
            ],
            compiler_params=pltpu.CompilerParams(
                collective_id=0, has_side_effects=True, vmem_limit_bytes=56 * 1024 * 1024
            ),
            cost_estimate=pl.CostEstimate(
                flops=HEADS * GROUP * CHIP * KEYS * DH * 12,
                bytes_accessed=5 * 1024 * 1024,
                transcendentals=HEADS * GROUP * CHIP * KEYS,
            ),
        )(queries, key_vectors, value_vectors, out_grad, doc_lengths.reshape(1, -1))
        return pl.pallas_call(
            copy_out,
            out_shape=(wide, wide, narrow, narrow),
            in_specs=[pl.BlockSpec(memory_space=pltpu.VMEM)] * 4,
            out_specs=(anywhere,) * 4,
            scratch_shapes=[dma((10,))],
            compiler_params=pltpu.CompilerParams(vmem_limit_bytes=8 * 1024 * 1024),
        )(*results)

    token = P(("cp", "hd"), None)
    return jax.shard_map(
        per_device,
        mesh=mesh,
        in_specs=(token, token, token, token, P()),
        out_specs=(token,) * 4,
        check_vma=False,
    )
```

```python
import functools
import math

import jax
import jax.numpy as jnp
from jax import lax
from jax.experimental import pallas as pl
from jax.experimental.pallas import tpu as pltpu
from jax.sharding import PartitionSpec as P

DH = 128
ROWS = 64
CHIP = 2 * ROWS
SLOTS = 5
KEYS = SLOTS * CHIP
HEADS = 4
GROUP = 8
WIDE = GROUP * DH
PAIR = 2 * CHIP
CHUNKS = GROUP // 2
SCALE = DH ** (-0.5)
MESH = pl.DeviceIdType.MESH
F32 = jnp.float32
BF16 = jnp.bfloat16


def kernel(
    devices,
    q_in, k_in, v_in, g_in, len_in,
    att_out, dq_out, dk_out, dv_out,
    kv, qb, gb, ob, dqb, acc, gin, gout, fin, bias, lens,
    value_t, grad_t, scores, tops, rows, probs, changes,
    k_own, v_own, q_away, g_away,
    len_sem, kv_recv, kv_fwd, own_ici, own_sib,
    qg_recv, qg_send, sum_recv, sum_send,
    out_send, out_recv, fin_send, fin_recv, kv_stage, qg_stage,
):
    cp = lax.axis_index("cp")
    hd = lax.axis_index("hd")
    me = cp * 8 + hd
    core = lax.rem(hd, 2)
    other = 1 - core

    def device(index):
        index = lax.rem(index + devices, devices)
        return (index // 8, lax.rem(index, 8))

    sibling = (cp, hd + 1 - 2 * core)
    chip_base = me - core
    chip = chip_base // 2
    not_last = chip < devices // 2 - 1
    ahead = device(me + 2)
    ahead_other = device(chip_base + 2 + other)
    behind = device(me - 2)
    behind_other = device(chip_base - 2 + other)
    my_rows = pl.ds(pl.multiple_of(core * ROWS, ROWS), ROWS)
    sib_rows = pl.ds(pl.multiple_of(other * ROWS, ROWS), ROWS)

    def head_cols(owner, h, width):
        return pl.ds(pl.multiple_of((owner * HEADS + h) * width, width), width)

    def remote(src, dst, send, recv, target):
        return pltpu.make_async_remote_copy(
            src_ref=src, dst_ref=dst, send_sem=send, recv_sem=recv, device_id=target, device_id_type=MESH
        )

    def own_to_ahead(h):
        made = []
        for part, src in enumerate((k_own, v_own)):
            for side, (owner, target) in enumerate(((core, ahead), (other, ahead_other))):
                made.append(remote(
                    src.at[:, head_cols(owner, h, DH)], kv.at[h, 3, part, my_rows],
                    own_ici.at[h, side, part], kv_recv.at[h, 3, part], target,
                ))
        return made

    def own_to_sibling(h):
        return [
            remote(src.at[:, head_cols(other, h, DH)], kv.at[h, 4, part, my_rows],
                   own_sib.at[h, part], kv_recv.at[h, 4, part], sibling)
            for part, src in enumerate((k_own, v_own))
        ]

    def own_local(h):
        return [
            pltpu.make_async_copy(src.at[:, head_cols(core, h, DH)], kv.at[h, 4, part, my_rows], kv_recv.at[h, 4, part])
            for part, src in enumerate((k_in, v_in))
        ]

    def rows_to_sibling(h):
        return [
            remote(src.at[h], dst.at[h, my_rows], qg_send.at[h, part], qg_recv.at[h, part], sibling)
            for part, (src, dst) in enumerate(((q_away, qb), (g_away, gb)))
        ]

    def stage_kv():
        return [
            pltpu.make_async_copy(src, dst, kv_stage.at[part])
            for part, (src, dst) in enumerate(((k_in, k_own), (v_in, v_own)))
        ]

    def stage_rows(h):
        return [
            pltpu.make_async_copy(src.at[:, head_cols(other, h, WIDE)], dst.at[h], qg_stage.at[h, part])
            for part, (src, dst) in enumerate(((q_in, q_away), (g_in, g_away)))
        ]

    def send_rows(h):
        for copy in stage_rows(h):
            copy.wait()
        start(rows_to_sibling(h))

    def rows_local(h):
        return [
            pltpu.make_async_copy(src.at[:, head_cols(core, h, WIDE)], dst.at[h, my_rows], qg_recv.at[h, part])
            for part, (src, dst) in enumerate(((q_in, qb), (g_in, gb)))
        ]

    def reaches(slot):
        return chip >= 4 - slot

    def start(copies):
        for copy in copies:
            copy.start()

    def wait_kv(h, slot, part):
        ref = kv.at[h, slot, part]
        pltpu.make_async_copy(ref, ref, kv_recv.at[h, slot, part]).wait()

    def wait_rows(h):
        for part, dst in enumerate((qb, gb)):
            pltpu.make_async_copy(dst.at[h], dst.at[h], qg_recv.at[h, part]).wait()

    def forward(h, slot, part):
        return remote(kv.at[h, slot, part], kv.at[h, slot - 1, part],
                      kv_fwd.at[h, slot - 1, part], kv_recv.at[h, slot - 1, part], ahead)

    def own_ahead(h):
        @pl.when(not_last)
        def _():
            start(own_to_ahead(h))

    def pass_on(h, slot, parts=(0, 1)):
        for part in parts:
            @pl.when(reaches(slot))
            def _():
                wait_kv(h, slot, part)

            @pl.when(reaches(slot) & not_last)
            def _():
                forward(h, slot, part).start()

    def sum_copy(h, slot, part):
        return remote(gout.at[h, slot, part], gin.at[h, slot, part],
                      sum_send.at[h, slot, part], sum_recv.at[h, slot, part], behind)

    def first_sum(h, part):
        gout[h, 0, part] = (acc[h, part, 0:CHIP] * (SCALE, 1.0)[part]).astype(BF16)
        @pl.when(reaches(0))
        def _():
            sum_copy(h, 0, part).start()

    def next_sum(h, part, slot):
        ref = gin.at[h, slot - 1, part]

        @pl.when(reaches(slot) & not_last)
        def _():
            pltpu.make_async_copy(ref, ref, sum_recv.at[h, slot - 1, part]).wait()

        mine = acc[h, part, slot * CHIP:(slot + 1) * CHIP] * (SCALE, 1.0)[part]
        total = gin[h, slot - 1, part].astype(F32) + mine
        if slot < 4:
            gout[h, slot, part] = total.astype(BF16)

            @pl.when(reaches(slot))
            def _():
                sum_copy(h, slot, part).start()
        else:
            fin[h, part] = total.astype(BF16)
            fin_remote(h, part).start()
            keep_fin(h, part)

    def keep_fin(h, part):
        (dk_out, dv_out)[part][:, head_cols(core, h, DH)] = fin[h, part, my_rows]

    def fin_remote(h, part):
        return remote(fin.at[h, part, sib_rows], (dk_out, dv_out)[part].at[:, head_cols(core, h, DH)],
                      fin_send.at[h, part], fin_recv.at[h, part], sibling)

    def out_remote(h, part):
        return remote((ob, dqb)[part].at[h, sib_rows], (att_out, dq_out)[part].at[:, head_cols(core, h, WIDE)],
                      out_send.at[h, part], out_recv.at[h, part], sibling)

    def give_out(h, part):
        out_remote(h, part).start()
        (att_out, dq_out)[part][:, head_cols(core, h, WIDE)] = (ob, dqb)[part][h, my_rows]

    for slot in range(4):
        @pl.when(chip < 4 - slot)
        def _():
            kv[:, slot] = jnp.zeros((HEADS, 2, CHIP, DH), BF16)

    @pl.when(chip == devices // 2 - 1)
    def _():
        gin[...] = jnp.zeros(gin.shape, BF16)

    barrier = pltpu.get_barrier_semaphore()
    for joined, peers in ((chip >= 0, (sibling,)), (not_last, (ahead, ahead_other)), (chip > 0, (behind, behind_other))):
        @pl.when(joined)
        def _():
            for peer in peers:
                pl.semaphore_signal(barrier, inc=1, device_id=peer, device_id_type=MESH)

    len_copy = pltpu.make_async_copy(len_in, lens, len_sem)
    len_copy.start()
    start(stage_kv())
    for h in range(HEADS):
        start(own_local(h))
        start(stage_rows(h))
        start(rows_local(h))
    for copy in stage_kv():
        copy.wait()
    pl.semaphore_wait(barrier, 1 + 2 * (not_last.astype(jnp.int32) + (chip > 0).astype(jnp.int32)))

    for h in range(2):
        own_ahead(h)
    for h in range(HEADS):
        start(own_to_sibling(h))
    send_rows(0)

    len_copy.wait()
    first_pos = (chip_base // 2) * CHIP
    low = lax.broadcasted_iota(jnp.int32, (DH, DH), 0)
    high = lax.broadcasted_iota(jnp.int32, (DH, DH), 1)
    ends_col = jnp.sum(jnp.where(high <= low, lens[...].astype(F32), 0.0), axis=1, keepdims=True)
    ends_row = jnp.sum(jnp.where(low == high, ends_col, 0.0), axis=0, keepdims=True)
    query_pos = high + first_pos
    query_seg = jnp.sum(jnp.where(ends_col <= query_pos.astype(F32), 1.0, 0.0), axis=0, keepdims=True)
    for slot in range(SLOTS):
        key_pos = low + (first_pos - (4 - slot) * CHIP)
        key_seg = jnp.sum(jnp.where(ends_row <= key_pos.astype(F32), 1.0, 0.0), axis=1, keepdims=True)
        allowed = (key_pos >= 0) & (key_pos <= query_pos) & (key_seg == query_seg)
        bias[slot * CHIP:(slot + 1) * CHIP, :] = jnp.where(allowed, 0.0, -1e30)

    pass_on(0, 3)
    send_rows(1)
    pass_on(1, 3)
    pass_on(0, 2)
    own_ahead(2)
    pass_on(1, 2)
    pass_on(0, 1)
    own_ahead(3)
    send_rows(2)
    pass_on(2, 3)
    pass_on(1, 1)
    send_rows(3)

    blocks = [slice(slot * CHIP, (slot + 1) * CHIP) for slot in range(SLOTS)]

    def cols_of(c):
        first = 2 * (c % CHUNKS)
        return [slice((first + i) * DH, (first + i + 1) * DH) for i in range(2)]

    def score_stage(c):
        h, side = c // CHUNKS, c % 2
        query = jnp.concatenate([qb[h, :, col].T for col in cols_of(c)], axis=1)
        raw = jnp.dot(kv[h, :, 0].reshape(KEYS, DH), query, preferred_element_type=F32)
        top = None
        for block in blocks:
            one_bias = bias[block]
            part = raw[block] * (SCALE * math.log2(math.e)) + jnp.concatenate([one_bias, one_bias], axis=1)
            scores[side, block] = part
            part = jnp.max(part.reshape(CHIP // 8, 8, PAIR), axis=0)
            top = part if top is None else jnp.maximum(top, part)
        tops[side] = top

    def weight_stage(c):
        side = c % 2
        top = jnp.max(tops[side], axis=0, keepdims=True)
        total = None
        for block in blocks:
            part = jnp.exp2(scores[side, block] - top)
            probs[c, block] = part.astype(BF16)
            part = jnp.sum(part.reshape(CHIP // 8, 8, PAIR), axis=0)
            total = part if total is None else total + part
        inverse = 1.0 / jnp.sum(total, axis=0, keepdims=True)
        inverse = jnp.broadcast_to(inverse, (CHIP, PAIR)).astype(BF16)
        for block in blocks:
            probs[c, block] = probs[c, block] * inverse

    def sum_stage(c, part):
        h = c // CHUNKS
        left, right = ((changes, qb), (probs, gb))[part]
        right = jnp.concatenate([right[h, :, col] for col in cols_of(c)], axis=0)
        total = jnp.dot(left[c], right, preferred_element_type=F32)
        if c % CHUNKS == 0:
            acc[h, part] = total
        else:
            acc[h, part] += total

    def out_stage(c):
        h, side = c // CHUNKS, c % 2
        out = jnp.dot(value_t[h % 2], probs[c], preferred_element_type=F32)
        cols = cols_of(c)
        grad = jnp.concatenate([gb[h, :, col].T for col in cols], axis=1)
        grad_t[side] = grad
        delta = jnp.sum(out.astype(BF16).astype(F32) * grad.astype(F32), axis=0, keepdims=True)
        rows[side] = jnp.broadcast_to(delta, (8, PAIR))
        out = out.T.astype(BF16)
        for i, col in enumerate(cols):
            ob[h, :, col] = out[i * CHIP:(i + 1) * CHIP]

    def change_stage(c):
        h, side = c // CHUNKS, c % 2
        raw = jnp.dot(kv[h, :, 1].reshape(KEYS, DH), grad_t[side], preferred_element_type=F32)
        delta = rows[side, 0:1]
        for block in blocks:
            changes[c, block] = probs[c, block] * (raw[block] - delta).astype(BF16)

    def query_stage(h):
        keys_t = kv[h, :, 0].reshape(KEYS, DH).T
        for c in range(h * CHUNKS, (h + 1) * CHUNKS):
            query_grad = (jnp.dot(keys_t, changes[c], preferred_element_type=F32) * SCALE).T.astype(BF16)
            for i, col in enumerate(cols_of(c)):
                dqb[h, :, col] = query_grad[i * CHIP:(i + 1) * CHIP]
        give_out(h, 1)

    def begin(h, part):
        if part == 0:
            wait_rows(h)
        wait_kv(h, 4, part)

        @pl.when(reaches(0))
        def _():
            wait_kv(h, 0, part)

        if part == 1:
            value_t[h % 2] = kv[h, :, 1].reshape(KEYS, DH).T

    def finish(h, part):
        first_sum(h, 1 - part)
        if part == 1:
            give_out(h, 0)

    def run(phases, after):
        items = [(h, part, h * CHUNKS + p) for h, part in phases for p in range(CHUNKS)]
        for step in range(len(items) + 2):
            if step < len(items):
                h, part, c = items[step]
                if c % CHUNKS == 0:
                    begin(h, part)
                (score_stage, out_stage)[part](c)
            if 0 <= step - 1 < len(items):
                h, part, c = items[step - 1]
                (weight_stage, change_stage)[part](c)
            if 0 <= step - 2:
                h, part, c = items[step - 2]
                sum_stage(c, 1 - part)
                if c % CHUNKS == CHUNKS - 1:
                    finish(h, part)
            for event, *where in after.get(step, []):
                event(*where)

    key, value = 0, 1
    run(((0, 0), (0, 1), (1, 0), (1, 1)), {
        5: [(pass_on, 2, 2, (key,)), (pass_on, 3, 3, (key,)), (pass_on, 2, 2, (value,)), (pass_on, 3, 3, (value,))],
        13: [(pass_on, 2, 1, (key,)), (pass_on, 3, 2, (key,)), (pass_on, 2, 1, (value,)), (pass_on, 3, 2, (value,))],
        14: [(next_sum, 0, value, 1)],
        17: [(next_sum, 0, key, 1)],
    })
    pass_on(3, 1)
    next_sum(1, value, 1)
    next_sum(0, value, 2)
    next_sum(1, key, 1)
    run(((2, 0), (3, 0), (2, 1), (3, 1)), {
        2: [(next_sum, 0, key, 2)],
        6: [(next_sum, 1, value, 2)],
        7: [(next_sum, 0, value, 3)],
        10: [(next_sum, 1, key, 2)],
        11: [(next_sum, 0, key, 3)],
        15: [(next_sum, 1, value, 3)],
        16: [(next_sum, 0, value, 4)],
        17: [(next_sum, 2, value, 1), (next_sum, 1, key, 3)],
    })
    for event, *where in (
        (next_sum, 0, key, 4), (next_sum, 3, value, 1), (query_stage, 0), (next_sum, 1, value, 4),
        (next_sum, 2, key, 1), (next_sum, 2, value, 2), (query_stage, 1), (next_sum, 1, key, 4),
        (next_sum, 3, key, 1), (next_sum, 3, value, 2), (query_stage, 2), (next_sum, 2, key, 2),
        (next_sum, 2, value, 3), (query_stage, 3), (next_sum, 3, key, 2), (next_sum, 3, value, 3),
        (next_sum, 2, key, 3), (next_sum, 2, value, 4), (next_sum, 3, key, 3), (next_sum, 3, value, 4),
        (next_sum, 2, key, 4), (next_sum, 3, key, 4),
    ):
        event(*where)

    for h in range(HEADS):
        for copy in own_to_sibling(h) + rows_to_sibling(h):
            copy.wait_send()

        @pl.when(not_last)
        def _():
            for copy in own_to_ahead(h):
                copy.wait_send()

        for slot in range(4):
            @pl.when(reaches(slot))
            def _():
                for part in range(2):
                    sum_copy(h, slot, part).wait_send()

        for slot in (3, 2, 1):
            @pl.when(reaches(slot) & not_last)
            def _():
                for part in range(2):
                    forward(h, slot, part).wait_send()

        for part in range(2):
            out_remote(h, part).wait_send()
            fin_remote(h, part).wait_send()
        for part, dst in enumerate((att_out, dq_out)):
            ref = dst.at[:, head_cols(other, h, WIDE)]
            pltpu.make_async_copy(ref, ref, out_recv.at[h, part]).wait()
        for part, dst in enumerate((dk_out, dv_out)):
            ref = dst.at[:, head_cols(other, h, DH)]
            pltpu.make_async_copy(ref, ref, fin_recv.at[h, part]).wait()


def copy_out(*refs):
    sources, targets, sem = refs[:4], refs[4:8], refs[8]
    copies = []
    for src, dst in zip(sources, targets):
        pieces = 4 if src.shape[1] > 1024 else 1
        step = src.shape[0] // pieces
        for piece in range(pieces):
            rows = pl.ds(piece * step, step)
            copies.append(pltpu.make_async_copy(src.at[rows], dst.at[rows], sem.at[len(copies)]))
    for copy in copies:
        copy.start()
    for copy in copies:
        copy.wait()


def solution(mesh):
    devices = mesh.shape["cp"] * mesh.shape["hd"]
    anywhere = pl.BlockSpec(memory_space=pl.ANY)
    dma = pltpu.SemaphoreType.DMA

    def per_device(queries, key_vectors, value_vectors, out_grad, doc_lengths):
        wide = jax.ShapeDtypeStruct(queries.shape, BF16)
        narrow = jax.ShapeDtypeStruct(key_vectors.shape, BF16)
        results = pl.pallas_call(
            functools.partial(kernel, devices),
            out_shape=tuple(pltpu.VMEM(x.shape, BF16) for x in (wide, wide, narrow, narrow)),
            in_specs=[anywhere] * 5,
            out_specs=(pl.BlockSpec(memory_space=pltpu.VMEM),) * 4,
            scratch_shapes=[
                pltpu.VMEM((HEADS, SLOTS, 2, CHIP, DH), BF16),
                pltpu.VMEM((HEADS, CHIP, WIDE), BF16),
                pltpu.VMEM((HEADS, CHIP, WIDE), BF16),
                pltpu.VMEM((HEADS, CHIP, WIDE), BF16),
                pltpu.VMEM((HEADS, CHIP, WIDE), BF16),
                pltpu.VMEM((HEADS, 2, KEYS, DH), F32),
                pltpu.VMEM((HEADS, 4, 2, CHIP, DH), BF16),
                pltpu.VMEM((HEADS, 4, 2, CHIP, DH), BF16),
                pltpu.VMEM((HEADS, 2, CHIP, DH), BF16),
                pltpu.VMEM((KEYS, DH), F32),
                pltpu.VMEM((1, 128), jnp.int32),
                pltpu.VMEM((2, DH, KEYS), BF16),
                pltpu.VMEM((2, DH, PAIR), BF16),
                pltpu.VMEM((2, KEYS, PAIR), F32),
                pltpu.VMEM((2, 8, PAIR), F32),
                pltpu.VMEM((2, 8, PAIR), F32),
                pltpu.VMEM((HEADS * CHUNKS, KEYS, PAIR), BF16),
                pltpu.VMEM((HEADS * CHUNKS, KEYS, PAIR), BF16),
                pltpu.VMEM((ROWS, 2 * HEADS * DH), BF16),
                pltpu.VMEM((ROWS, 2 * HEADS * DH), BF16),
                pltpu.VMEM((HEADS, ROWS, WIDE), BF16),
                pltpu.VMEM((HEADS, ROWS, WIDE), BF16),
                dma,
                dma((HEADS, SLOTS, 2)),
                dma((HEADS, 3, 2)),
                dma((HEADS, 2, 2)),
                dma((HEADS, 2)),
                dma((HEADS, 2)),
                dma((HEADS, 2)),
                dma((HEADS, 4, 2)),
                dma((HEADS, 4, 2)),
                dma((HEADS, 2)),
                dma((HEADS, 2)),
                dma((HEADS, 2)),
                dma((HEADS, 2)),
                dma((2,)),
                dma((HEADS, 2)),
            ],
            compiler_params=pltpu.CompilerParams(
                collective_id=0, has_side_effects=True, vmem_limit_bytes=56 * 1024 * 1024
            ),
            cost_estimate=pl.CostEstimate(
                flops=HEADS * GROUP * CHIP * KEYS * DH * 12,
                bytes_accessed=5 * 1024 * 1024,
                transcendentals=HEADS * GROUP * CHIP * KEYS,
            ),
        )(queries, key_vectors, value_vectors, out_grad, doc_lengths.reshape(1, -1))
        return pl.pallas_call(
            copy_out,
            out_shape=(wide, wide, narrow, narrow),
            in_specs=[pl.BlockSpec(memory_space=pltpu.VMEM)] * 4,
            out_specs=(anywhere,) * 4,
            scratch_shapes=[dma((10,))],
            compiler_params=pltpu.CompilerParams(vmem_limit_bytes=8 * 1024 * 1024),
        )(*results)

    token = P(("cp", "hd"), None)
    return jax.shard_map(
        per_device,
        mesh=mesh,
        in_specs=(token, token, token, token, P()),
        out_specs=(token,) * 4,
        check_vma=False,
    )
```
